128 devices in a mesh: face: 32 (over z, x, core), tile: 4 (over y).
Axes of the slice: x: 4, y: 4, z: 4, core: 2. Of those that a mesh axis runs over, the one named last changes fastest.
Arguments:
- latlon: bfloat16 [524288, 256], P(('face', 'tile')), may hold values from -6 to 6
- send_rows: int32 [128, 8, 1024], P(('face', 'tile')), may hold values from 0 to 4095
- send_count: int32 [128, 8], P(('face', 'tile')), may hold values from 1 to 1024, as said below
- interp_slot: int32 [131072, 4], P(('face', 'tile')), may hold values from 0 to 8191, as said below
- interp_weight: float32 [131072, 4], P(('face', 'tile')), may hold values from 0.1 to 1
- outer_partner: int32 [32, 4, 2], P('face', 'tile'), may hold values from 0 to 31, as said below
- outer_side: int32 [32, 4, 2], P('face', 'tile'), may hold values from 0 to 1
- outer_flip: int32 [32, 4, 2], P('face', 'tile'), may hold values from 0 to 1
- conv_weight: bfloat16 [3, 3, 256, 256], replicated, may hold values from -0.125 to 0.125
- conv_bias: float32 [256], replicated, may hold values from -3 to 3
- cotangent: bfloat16 [131072, 256], P(('face', 'tile')), may hold values from -6 to 6
Outputs:
- activated: bfloat16 [131072, 256], P(('face', 'tile'))
- grad_latlon: bfloat16 [524288, 256], P(('face', 'tile'))
- grad_weight: float32 [3, 3, 256, 256], replicated
- grad_bias: float32 [256], replicated
The draws below stay inside these ranges and needn't reach their ends.
Inputs may be any that keep to these rules, and one draw needn't show every extreme that they name: `send_count`: each source device fills all 1024 slots of at least one slot group, and one tile receives 1024 rows from every one of its 8 source devices. `send_rows`: A row of the source device's own lat-lon rows; only slots below send_count carry data. `interp_slot`: every entry of a pixel of tile d is n * 1024 + j with j < send_count[(d + n - 4) mod 128, n]. `outer_partner`: outer slots pair up among tiles of the same quarter index: if slot s of (f, t) names slot e of (g, t), then slot e of (g, t) names slot s of (f, t), and outer_flip is the same for both; no slot names itself.
All inputs are finite; a program needn't handle non-finite values.
Results may differ from the reference program's by a relative error of at most 0.0075.
Values may be sent and summed in bfloat16 or wider, within the bound.
No kernel may reach another device: no remote copies, remote signals or barrier semaphores. Data moves between devices by JAX's collectives and lax.ppermute only.
A program may use at most 128 MiB of HBM per device.

```python
import math
import jax
import jax.numpy as jnp
from jax import lax

C = 256
TS = 32
LL_DEV = 4096
K = 4
NEAR = 8
CAP = 1024
FACE_BLOCKS = 32
QUARTERS = 4
TILES = 128
PIX = 1024


def shared_counts(key):
    base_key = jax.random.fold_in(key, 71)
    upper_key, fill_key, full_key, polar_key = jax.random.split(base_key, 4)
    sources = jnp.arange(TILES, dtype=jnp.int32)[:, None]
    groups = jnp.arange(NEAR, dtype=jnp.int32)[None, :]
    targets = (sources - groups + NEAR // 2) % TILES
    upper = jax.random.randint(upper_key, (TILES,), max(CAP // 4, 1), CAP + 1)
    upper_here = upper[targets]
    lower = jnp.maximum(upper_here // 2, 1)
    fraction = jax.random.randint(fill_key, (TILES, NEAR), 0, 1024)
    counts = lower + fraction * (upper_here - lower + 1) // 1024
    full_group = jax.random.randint(full_key, (TILES,), 0, NEAR)
    polar_tile = jax.random.randint(polar_key, (), 0, TILES)
    counts = jnp.where(groups == full_group[:, None], CAP, counts)
    counts = jnp.where(targets == polar_tile, CAP, counts)
    return counts.astype(jnp.int32)


def shared_pairing(key):
    base_key = jax.random.fold_in(key, 301)
    slot_total = 2 * FACE_BLOCKS
    key_list = jax.random.split(base_key, QUARTERS + 1)
    orders = jax.vmap(lambda sub_key: jax.random.permutation(sub_key, slot_total))(key_list[:QUARTERS])
    positions = jnp.argsort(orders, axis=1)
    mates = jnp.take_along_axis(orders, positions ^ 1, axis=1)
    pair_flips = jax.random.randint(key_list[QUARTERS], (QUARTERS, FACE_BLOCKS), 0, 2)
    flips = jnp.take_along_axis(pair_flips, positions // 2, axis=1)
    mates = mates.reshape(QUARTERS, FACE_BLOCKS, 2).transpose(1, 0, 2)
    flips = flips.reshape(QUARTERS, FACE_BLOCKS, 2).transpose(1, 0, 2)
    return (mates.astype(jnp.int32), flips.astype(jnp.int32))


def draw_send_count(key, part):
    return shared_counts(key)


def draw_interp_slot(key, part):
    counts = shared_counts(key)
    own_key = jax.random.fold_in(key, 5)
    group_key, slot_key = jax.random.split(own_key)
    destination = (jnp.arange(TILES * PIX, dtype=jnp.int32) // PIX)[:, None]
    group = jax.random.randint(group_key, (TILES * PIX, K), 0, NEAR)
    source_tile = (destination + group - NEAR // 2) % TILES
    live_count = counts[source_tile, group]
    slot_number = jax.random.randint(slot_key, (TILES * PIX, K), 0, 1 << 20) % live_count
    return (group * CAP + slot_number).astype(jnp.int32)


def draw_outer_partner(key, part):
    mates, flips = shared_pairing(key)
    return (mates // 2).astype(jnp.int32)


def draw_outer_side(key, part):
    mates, flips = shared_pairing(key)
    return (mates % 2).astype(jnp.int32)


def draw_outer_flip(key, part):
    mates, flips = shared_pairing(key)
    return flips


def plant(result, rng, least, high):
    longest = result.shape.index(max(result.shape))
    spots = []
    for shift in (0, 1):
        where = [jax.random.randint(jax.random.fold_in(rng, axis), (), 0, length) for axis, length in enumerate(result.shape)]
        where[longest] = (where[longest] + shift) % result.shape[longest]
        spots.append(tuple(where))
    return result.at[spots[0]].set(least).at[spots[1]].set(high)


def shard_levels(key, shape, cuts, least, top_value):
    factor_of = 1.0
    for dim, shards_of in cuts:
        draws = jax.random.uniform(jax.random.fold_in(jax.random.fold_in(key, 6), dim), (shards_of,), jnp.float32, least / len(cuts), top_value / len(cuts))
        factor_of = factor_of * jnp.repeat(jnp.exp(draws), shape[dim] // shards_of).reshape((-1,) + (1,) * (len(shape) - 1 - dim))
    return factor_of


def gaussian(key, dims, scale, bound, pieces=(), held_as=jnp.bfloat16):
    values = scale * jax.random.normal(key, dims, jnp.float32)
    if pieces:
        values = values * shard_levels(key, dims, pieces, -0.22, 0.18)
    return jnp.clip(values, -bound, bound).astype(held_as)


def setup_inputs(seed: int = 0) -> dict:
    streams_of = jax.random.split(jax.random.key(seed), 12)
    return {
        "latlon": gaussian(streams_of[0], (TILES * LL_DEV, C), 1.0, 6.0, ((0, 128),)),
        "send_rows": plant(jax.random.randint(streams_of[1], (TILES, NEAR, CAP), 0, LL_DEV), jax.random.fold_in(streams_of[1], 1), 0, LL_DEV - 1).astype(jnp.int32),
        "send_count": draw_send_count(jax.random.fold_in(streams_of[11], 71), 0),
        "interp_slot": draw_interp_slot(jax.random.fold_in(streams_of[11], 71), 0),
        "interp_weight": jnp.clip(jnp.exp(math.log(1.0) - 2.3025851 * jax.random.uniform(streams_of[4], (TILES * PIX, K), jnp.float32) ** shard_levels(streams_of[4], (TILES * PIX, K), ((0, 128),), -0.2, 0.2)), 0.1, 1.0),
        "outer_partner": draw_outer_partner(jax.random.fold_in(streams_of[11], 71), 0),
        "outer_side": draw_outer_side(jax.random.fold_in(streams_of[11], 71), 0),
        "outer_flip": draw_outer_flip(jax.random.fold_in(streams_of[11], 71), 0),
        "conv_weight": gaussian(streams_of[8], (3, 3, C, C), (9 * C) ** -0.5, 0.125),
        "conv_bias": gaussian(streams_of[9], (C,), 0.5, 3.0, (), jnp.float32),
        "cotangent": gaussian(streams_of[10], (TILES * PIX, C), 1.0, 6.0, ((0, 128),)),
    }


root_half = 0.7071067811865476
inv_root_two_pi = 0.3989422804014327


def gelu_parts(pre):
    normal_cdf = 0.5 * (1.0 + lax.erf(pre * root_half))
    return pre * normal_cdf, normal_cdf + pre * inv_root_two_pi * jnp.exp(-0.5 * pre * pre)


def pad_tile(grid, north_cycle, south_cycle, west_cycle, east_cycle):
    padded = jnp.pad(grid, ((1, 1), (1, 1), (0, 0)))
    padded = padded.at[0, 1:-1].set(north_cycle)
    padded = padded.at[-1, 1:-1].set(south_cycle)
    padded = padded.at[1:-1, 0].set(west_cycle)
    padded = padded.at[1:-1, -1].set(east_cycle)
    return padded


def convolve(padded, conv_weight, conv_bias):
    extent = padded.shape[0] - 2
    channels = padded.shape[-1]
    summed = jnp.zeros((extent * extent, conv_weight.shape[-1]), jnp.float32) + conv_bias[None, :]
    for tap_row in range(3):
        for tap_col in range(3):
            window = padded[tap_row:tap_row + extent, tap_col:tap_col + extent].reshape(extent * extent, channels)
            summed = summed + jnp.dot(window, conv_weight[tap_row, tap_col], preferred_element_type=jnp.float32)
    return summed


def backward_tile(padded, pre, cotangent, conv_weight):
    extent = padded.shape[0] - 2
    channels = padded.shape[-1]
    activated, slope = gelu_parts(pre)
    grad_pre = (cotangent.astype(jnp.float32) * slope).astype(jnp.bfloat16)
    weight_terms = []
    grad_padded = jnp.zeros(padded.shape, jnp.float32)
    for tap_row in range(3):
        for tap_col in range(3):
            window = padded[tap_row:tap_row + extent, tap_col:tap_col + extent].reshape(extent * extent, channels)
            weight_terms.append(lax.dot_general(window, grad_pre, (((0,), (0,)), ((), ())), preferred_element_type=jnp.float32))
            spread = lax.dot_general(grad_pre, conv_weight[tap_row, tap_col], (((1,), (1,)), ((), ())), preferred_element_type=jnp.float32)
            grad_padded = grad_padded + jnp.pad(spread.reshape(extent, extent, channels), ((tap_row, 2 - tap_row), (tap_col, 2 - tap_col), (0, 0)))
    grad_weight = jnp.stack(weight_terms).reshape(3, 3, channels, channels)
    grad_bias = jnp.sum(grad_pre.astype(jnp.float32), axis=0)
    return activated.astype(jnp.bfloat16), grad_weight, grad_bias, grad_padded


def cycle_lines(grad_padded):
    return jnp.stack([grad_padded[0, 1:-1], grad_padded[-1, 1:-1], grad_padded[1:-1, 0], grad_padded[1:-1, -1]]).astype(jnp.bfloat16)


def add_strips(grid_grad, inner_rows, inner_cols, outer_rows, outer_cols, top_row, left_col):
    final_index = grid_grad.shape[0] - 1
    grid_grad = grid_grad.at[jnp.where(top_row, final_index, 0)].add(inner_rows.astype(jnp.float32))
    grid_grad = grid_grad.at[:, jnp.where(left_col, final_index, 0)].add(inner_cols.astype(jnp.float32))
    grid_grad = grid_grad.at[jnp.where(top_row, 0, final_index)].add(outer_rows.astype(jnp.float32))
    grid_grad = grid_grad.at[:, jnp.where(left_col, 0, final_index)].add(outer_cols.astype(jnp.float32))
    return grid_grad


def route_edges(north, south, west, east, top_rows, left_cols, outer_partner, outer_side, outer_flip):
    quarter_ids = jnp.arange(QUARTERS, dtype=jnp.int32)
    inner_rows = jnp.where(top_rows, south, north)[:, quarter_ids ^ 2]
    inner_cols = jnp.where(left_cols, east, west)[:, quarter_ids ^ 1]
    outer = jnp.stack([jnp.where(top_rows, north, south), jnp.where(left_cols, west, east)], axis=2)
    chosen = outer[outer_partner, quarter_ids[None, :, None], outer_side]
    routed = jnp.where((outer_flip == 1)[:, :, :, None, None], chosen[:, :, :, ::-1], chosen)
    return inner_rows, inner_cols, routed[:, :, 0], routed[:, :, 1]


def reference(latlon, send_rows, send_count, interp_slot, interp_weight, outer_partner, outer_side, outer_flip, conv_weight, conv_bias, cotangent):
    tile_total = FACE_BLOCKS * QUARTERS
    pixel_total = TS * TS
    source_rows = latlon.reshape(tile_total, LL_DEV, C)
    slot_index = jnp.arange(CAP, dtype=jnp.int32)
    tile_index = jnp.arange(tile_total, dtype=jnp.int32)
    group_ids = jnp.arange(NEAR, dtype=jnp.int32)
    slots_by_tile = interp_slot.reshape(tile_total, pixel_total, K)
    weights_by_tile = interp_weight.reshape(tile_total, pixel_total, K)

    def sources_of(which_tile):
        return ((which_tile + group_ids - NEAR // 2) % tile_total).astype(jnp.int32)

    def interpolate(which_tile):
        sources = sources_of(which_tile)
        picked = source_rows[sources[:, None], send_rows[sources, group_ids]]
        live_mask = slot_index[None, :] < send_count[sources, group_ids][:, None]
        lookup_rows = jnp.where(live_mask[:, :, None], picked, jnp.zeros_like(picked)).reshape(NEAR * CAP, C)
        slots = slots_by_tile[which_tile]
        weights = weights_by_tile[which_tile]
        summed = jnp.zeros((pixel_total, C), jnp.float32)
        for neighbor in range(K):
            summed = summed + weights[:, neighbor, None] * lookup_rows[slots[:, neighbor]].astype(jnp.float32)
        return summed.astype(jnp.bfloat16)

    field = lax.map(interpolate, tile_index).reshape(FACE_BLOCKS, QUARTERS, TS, TS, C)
    quarter_ids = jnp.arange(QUARTERS, dtype=jnp.int32)
    top_rows = (quarter_ids // 2 == 0)[None, :, None, None]
    left_cols = (quarter_ids % 2 == 0)[None, :, None, None]
    inner_rows, inner_cols, outer_rows, outer_cols = route_edges(field[:, :, 0], field[:, :, -1], field[:, :, :, 0], field[:, :, :, -1], top_rows, left_cols, outer_partner, outer_side, outer_flip)
    north_cycle = jnp.where(top_rows, outer_rows, inner_rows)
    south_cycle = jnp.where(top_rows, inner_rows, outer_rows)
    west_cycle = jnp.where(left_cols, outer_cols, inner_cols)
    east_cycle = jnp.where(left_cols, inner_cols, outer_cols)
    cycles = jnp.stack([north_cycle, south_cycle, west_cycle, east_cycle], axis=2).reshape(tile_total, 4, TS, C)
    grids = field.reshape(tile_total, TS, TS, C)
    cot_tiles = cotangent.reshape(tile_total, pixel_total, C)

    def forward_step(totals, inputs):
        grid, cycle_set, grad_out = inputs
        padded = pad_tile(grid, cycle_set[0], cycle_set[1], cycle_set[2], cycle_set[3])
        pre = convolve(padded, conv_weight, conv_bias)
        activated, weight_part, bias_part, grad_padded = backward_tile(padded, pre, grad_out, conv_weight)
        return (totals[0] + weight_part, totals[1] + bias_part), (activated, grad_padded[1:-1, 1:-1], cycle_lines(grad_padded))

    start_totals = (jnp.zeros((3, 3, C, C), jnp.float32), jnp.zeros((C,), jnp.float32))
    (grad_weight, grad_bias), (activated, interiors, cycle_grads) = lax.scan(forward_step, start_totals, (grids, cycles, cot_tiles))
    cycle_grads = cycle_grads.reshape(FACE_BLOCKS, QUARTERS, 4, TS, C)
    strip_parts = route_edges(cycle_grads[:, :, 0], cycle_grads[:, :, 1], cycle_grads[:, :, 2], cycle_grads[:, :, 3], top_rows, left_cols, outer_partner, outer_side, outer_flip)
    strip_grads = jnp.stack(strip_parts, axis=2).reshape(tile_total, 4, TS, C)

    def gradient_step(grad_rows, inputs):
        which_tile, interior, strips = inputs
        quarter = which_tile % QUARTERS
        grid_grad = add_strips(interior, strips[0], strips[1], strips[2], strips[3], quarter // 2 == 0, quarter % 2 == 0)
        flat_grad = grid_grad.reshape(pixel_total, C)
        slots = slots_by_tile[which_tile]
        weights = weights_by_tile[which_tile]
        table_grad = jnp.zeros((NEAR * CAP, C), jnp.float32)
        for neighbor in range(K):
            table_grad = table_grad.at[slots[:, neighbor]].add(weights[:, neighbor, None] * flat_grad)
        table_grad = table_grad.astype(jnp.bfloat16).reshape(NEAR, CAP, C)
        sources = sources_of(which_tile)
        live_mask = slot_index[None, :] < send_count[sources, group_ids][:, None]
        targets = (sources[:, None] * LL_DEV + send_rows[sources, group_ids]).astype(jnp.int32)
        masked = jnp.where(live_mask[:, :, None], table_grad, jnp.zeros_like(table_grad)).astype(jnp.float32)
        return grad_rows.at[targets.reshape(-1)].add(masked.reshape(-1, C)), None

    grad_rows, unused = lax.scan(gradient_step, jnp.zeros((tile_total * LL_DEV, C), jnp.float32), (tile_index, interiors, strip_grads))
    return activated.reshape(tile_total * pixel_total, C), grad_rows.astype(jnp.bfloat16), grad_weight, grad_bias
```

```python
import functools
import jax
import jax.numpy as jnp
from jax import lax
from jax.experimental import pallas as pl
from jax.experimental.pallas import tpu as pltpu
from jax.sharding import PartitionSpec as P

BF = jnp.bfloat16
F32 = jnp.float32
I16 = jnp.int16
I32 = jnp.int32
AXES = ("face", "tile")
TS = 32
PIX = 1024
CAP = 1024
ROWS = 4096
C = 256
MT = 512
KC = 256

root_half = 0.7071067811865476
inv_root_two_pi = 0.3989422804014327
VM = pl.BlockSpec(memory_space=pltpu.VMEM)
SM = pl.BlockSpec(memory_space=pltpu.SMEM)
HB = pl.BlockSpec(memory_space=pl.ANY)
NT = (((1,), (1,)), ((), ()))


def params(mib):
    return pltpu.CompilerParams(vmem_limit_bytes=mib * 2**20)


def cost(flops, size):
    return pl.CostEstimate(flops=flops, bytes_accessed=size, transcendentals=0)


def far_face(j, k):
    return 1 if k == 0 or j + k >= 4 else -1


def to_far(value, k, faces):
    pairs = []
    for face in range(faces):
        for j in range(4):
            pairs.append((face * 4 + j, (face + far_face(j, k)) % faces * 4 + j))
    return lax.ppermute(value, AXES, pairs)


def from_far(value, k, faces):
    pairs = []
    for face in range(faces):
        for j in range(4):
            pairs.append(((face + far_face(j, k)) % faces * 4 + j, face * 4 + j))
    return lax.ppermute(value, AXES, pairs)


def from_far_tile(value, k, faces):
    pairs = []
    for face in range(faces):
        for j in range(4):
            pairs.append(((face + far_face(j, k)) % faces * 4 + (j + k) % 4, face * 4 + j))
    return lax.ppermute(value, AXES, pairs)


def along_tile(value, k):
    return lax.ppermute(value, "tile", [(i, (i + k) % 4) for i in range(4)])


def along_x(value, k):
    return lax.ppermute(value, "face", [(i, (i & ~6) | ((((i >> 1) + k) & 3) << 1)) for i in range(32)])


def along_z(value, k):
    return lax.ppermute(value, "face", [(i, (i + 8 * k) % 32) for i in range(32)])


def other_core(value):
    return lax.ppermute(value, "face", [(i, i ^ 1) for i in range(32)])


def lanes_iota(shape, dim, dtype):
    return lax.broadcasted_iota(I32, shape, dim).astype(dtype)


def gather_kernel(blocks, has_add, idx_ref, meta_ref, table_ref, *rest):
    if has_add:
        add_ref, out_ref, got_ref = rest
    else:
        out_ref, got_ref = rest
    base = lanes_iota((MT, KC), 1, I16)
    one = jnp.ones((MT, KC), BF)
    zero = jnp.zeros((MT, KC), BF)
    reps = KC // 128

    def spread(col, dtype):
        wide = jnp.broadcast_to(col, (MT, 128)).astype(dtype)
        return jnp.concatenate([wide] * reps, axis=1)

    for b in range(blocks):
        def pick(m, carry):
            rows = pl.ds(pl.multiple_of(m * MT, MT), MT)
            want = spread(idx_ref[rows, b : b + 1], I16)
            acc = jnp.zeros((MT, C), F32)
            for k in range(ROWS // KC):
                hot = jnp.where(want == base + jnp.asarray(k * KC, I16), one, zero)
                acc = acc + jnp.dot(hot, table_ref[k * KC : (k + 1) * KC, :], preferred_element_type=F32)
            got_ref[rows, :] = acc.astype(BF)
            return carry

        lax.fori_loop(0, CAP // MT, pick, 0)

        def mix(m, carry):
            rows = pl.ds(pl.multiple_of(m * MT, MT), MT)
            slots = [spread(meta_ref[b, rows, k : k + 1], I16) for k in range(4)]
            scale = [spread(meta_ref[b, rows, 4 + k : 5 + k], BF) for k in range(4)]
            acc = add_ref[b, rows, :].astype(F32) if has_add else jnp.zeros((MT, C), F32)
            for q in range(CAP // KC):
                here = base + jnp.asarray(q * KC, I16)
                w = jnp.where(slots[0] == here, scale[0], zero)
                for k in range(1, 4):
                    w = w + jnp.where(slots[k] == here, scale[k], zero)
                acc = acc + jnp.dot(w, got_ref[q * KC : (q + 1) * KC, :], preferred_element_type=F32)
            out_ref[b, rows, :] = acc.astype(BF)
            return carry

        lax.fori_loop(0, PIX // MT, mix, 0)


def partial_sums(idx, meta, table, add=None):
    blocks = idx.shape[1]
    has_add = add is not None
    operands = (idx, meta, table) + ((add,) if has_add else ())
    return pl.pallas_call(
        functools.partial(gather_kernel, blocks, has_add),
        out_shape=jax.ShapeDtypeStruct((blocks, PIX, C), BF),
        in_specs=[VM] * len(operands),
        out_specs=VM,
        scratch_shapes=[pltpu.VMEM((CAP, C), BF)],
        compiler_params=params(40),
        cost_estimate=cost(blocks * 2 * 5 * 2**28 * 2, 2**21),
    )(*operands)


def scatter_kernel(blocks, has_add, idx_ref, meta_ref, *rest):
    grads = rest[:blocks]
    rest = rest[blocks:]
    if has_add:
        add_ref, out_ref, slot_ref = rest
    else:
        out_ref, slot_ref = rest
    base = lanes_iota((MT, KC), 0, I16)
    one = jnp.ones((MT, KC), BF)
    zero = jnp.zeros((MT, KC), BF)

    def spread(row, dtype):
        tall = jnp.broadcast_to(row, (16, KC)).astype(dtype)
        return jnp.broadcast_to(tall[None], (MT // 16, 16, KC)).reshape(MT, KC)

    for b in range(blocks):
        def mix(m, carry):
            first = (m * MT).astype(F32)
            acc = jnp.zeros((MT, C), F32)
            for q in range(PIX // KC):
                lanes = slice(q * KC, (q + 1) * KC)
                w = None
                for k in range(4):
                    slots = spread((meta_ref[b, k : k + 1, lanes] - first).astype(I32), I16)
                    term = jnp.where(slots == base, spread(meta_ref[b, 4 + k : 5 + k, lanes], BF), zero)
                    w = term if w is None else w + term
                acc = acc + jnp.dot(w, grads[b][lanes, :], preferred_element_type=F32)
            slot_ref[pl.ds(pl.multiple_of(b * CAP + m * MT, MT), MT), :] = acc.astype(BF)
            return carry

        lax.fori_loop(0, CAP // MT, mix, 0)

    def put(m, carry):
        rows = pl.ds(pl.multiple_of(m * MT, MT), MT)
        acc = add_ref[rows, :] if has_add else jnp.zeros((MT, C), F32)
        for b in range(blocks):
            for q in range(CAP // KC):
                want = spread(idx_ref[b : b + 1, q * KC : (q + 1) * KC] - m * MT, I16)
                hot = jnp.where(want == base, one, zero)
                acc = acc + jnp.dot(
                    hot, slot_ref[b * CAP + q * KC : b * CAP + (q + 1) * KC, :], preferred_element_type=F32
                )
        out_ref[rows, :] = acc.astype(out_ref.dtype)
        return carry

    lax.fori_loop(0, ROWS // MT, put, 0)


def row_grads(idx, meta, grads, add, dtype):
    blocks = idx.shape[0]
    has_add = add is not None
    operands = (idx, meta) + tuple(grads) + ((add,) if has_add else ())
    return pl.pallas_call(
        functools.partial(scatter_kernel, blocks, has_add),
        out_shape=jax.ShapeDtypeStruct((ROWS, C), dtype),
        in_specs=[VM] * len(operands),
        out_specs=VM,
        scratch_shapes=[pltpu.VMEM((blocks * CAP, C), BF)],
        compiler_params=params(40),
        cost_estimate=cost(blocks * 2 * 5 * 2**28 * 2, 2**22),
    )(*operands)


def spread_rows(lines):
    rows = lines.shape[0]
    return jnp.broadcast_to(lines[:, None, :], (rows, TS, C)).reshape(rows * TS, C)


def split_lines(flags, north, south, west, east, inner_ref, outer_ref):
    top = flags[6] == 1
    left = flags[7] == 1
    inner_ref[0] = jnp.where(top, south, north).astype(BF)
    inner_ref[1] = jnp.where(left, east, west).astype(BF)
    outer_ref[0] = jnp.where(top, north, south).astype(BF)
    outer_ref[1] = jnp.where(left, west, east).astype(BF)


def outer_copies(flags, near_ref, far_ref, buf_ref, sem):
    for s in range(2):
        @pl.when(flags[8 + s] == 0)
        def _():
            pltpu.make_async_copy(near_ref.at[flags[s], flags[2 + s]], buf_ref.at[s], sem.at[s]).start()

        @pl.when(flags[8 + s] != 0)
        def _():
            pltpu.make_async_copy(far_ref.at[flags[s], flags[2 + s]], buf_ref.at[s], sem.at[s]).start()
    for s in range(2):
        pltpu.make_async_copy(near_ref.at[0, 0], buf_ref.at[s], sem.at[s]).wait()


def join_lines(flags, inner_ref, buf_ref):
    row = lax.broadcasted_iota(I32, (TS, TS), 0)
    col = lax.broadcasted_iota(I32, (TS, TS), 1)
    turn = (row + col == TS - 1).astype(BF)
    outer = []
    for s in range(2):
        line = buf_ref[s]
        back = jnp.dot(turn, line, preferred_element_type=F32)
        outer.append(jnp.where(flags[4 + s] == 1, back, line.astype(F32)))
    top = flags[6] == 1
    left = flags[7] == 1
    in_rows = inner_ref[0].astype(F32)
    in_cols = inner_ref[1].astype(F32)
    north = jnp.where(top, outer[0], in_rows)
    south = jnp.where(top, in_rows, outer[0])
    west = jnp.where(left, outer[1], in_cols)
    east = jnp.where(left, in_cols, outer[1])
    return north, south, west, east


def exchange(inner, outer):
    rows = lax.ppermute(inner[0], "tile", [(i, i ^ 2) for i in range(4)])
    cols = lax.ppermute(inner[1], "tile", [(i, i ^ 1) for i in range(4)])
    line = jnp.stack([outer] + [along_x(outer, k) for k in (1, 2, 3)])
    plane = jnp.concatenate([line] + [along_z(line, k) for k in (1, 2, 3)])
    return jnp.stack([rows, cols]), plane, other_core(plane)


EDGE_SCRATCH = [pltpu.VMEM((2, TS, C), BF), pltpu.SemaphoreType.DMA((2,))]
LINES = [jax.ShapeDtypeStruct((2, TS, C), BF)] * 2


def field_kernel(flags, a_ref, b_ref, c_ref, d_ref, field_ref, inner_ref, outer_ref):
    total = a_ref[...].astype(F32) + b_ref[...].astype(F32) + c_ref[...].astype(F32) + d_ref[...].astype(F32)
    field_ref[...] = total.astype(BF)
    grid = total.reshape(TS, TS, C)
    split_lines(flags, total[0:TS], total[PIX - TS : PIX], grid[:, 0, :], grid[:, TS - 1, :], inner_ref, outer_ref)


def make_field(flags, parts):
    return pl.pallas_call(
        field_kernel,
        out_shape=[jax.ShapeDtypeStruct((PIX, C), BF)] + LINES,
        in_specs=[SM] + [VM] * 4,
        out_specs=[VM] * 3,
        compiler_params=params(24),
        cost_estimate=cost(2**20, 3 * 2**20),
    )(flags, *parts)


def conv_kernel(flags, field_ref, in_ref, near_ref, far_ref, w_ref, bias_ref, cot_ref,
                act_ref, gp_ref, p_ref, mid_ref, inner_ref, outer_ref, q_ref, gf_ref, buf_ref, sem):
    n = 34 * TS
    outer_copies(flags, near_ref, far_ref, buf_ref, sem)
    north, south, west, east = join_lines(flags, in_ref, buf_ref)
    zero = jnp.zeros((1, C), F32)
    p_ref[1, 0:TS, :] = north.astype(BF)
    p_ref[1, TS : TS + PIX, :] = field_ref[...]
    p_ref[1, TS + PIX : n, :] = south.astype(BF)
    x = p_ref[1].astype(F32)
    col = lax.broadcasted_iota(I32, (n, C), 0) % TS
    west = jnp.concatenate([zero, west, zero])
    east = jnp.concatenate([zero, east, zero])
    p_ref[0] = jnp.where(col == 0, spread_rows(west), pltpu.roll(x, 1, 0)).astype(BF)
    p_ref[2] = jnp.where(col == TS - 1, spread_rows(east), pltpu.roll(x, n - 1, 0)).astype(BF)
    step = 256
    q_ref[1, 0 : 2 * TS, :] = jnp.zeros((2 * TS, C), BF)
    q_ref[1, 2 * TS + PIX : 4 * TS + PIX, :] = jnp.zeros((2 * TS, C), BF)
    for m in range(PIX // step):
        rows = slice(m * step, (m + 1) * step)
        pre = jnp.broadcast_to(bias_ref[...], (step, C))
        for a in range(3):
            for b in range(3):
                pre = pre + jnp.dot(
                    p_ref[b, a * TS + m * step : a * TS + (m + 1) * step, :], w_ref[a, b], preferred_element_type=F32
                )
        cdf = 0.5 * (1.0 + lax.erf(pre * root_half))
        act_ref[rows, :] = (pre * cdf).astype(BF)
        slope = cdf + pre * inv_root_two_pi * jnp.exp(-0.5 * pre * pre)
        g = (cot_ref[rows, :].astype(F32) * slope).astype(BF)
        gp_ref[rows, :] = g
        q_ref[1, 2 * TS + m * step : 2 * TS + (m + 1) * step, :] = g
        gf_ref[rows, :] = g.astype(F32)
    nq = 36 * TS
    y = q_ref[1].astype(F32)
    colq = lax.broadcasted_iota(I32, (nq, C), 0) % TS
    q_ref[0] = jnp.where(colq == TS - 1, 0.0, pltpu.roll(y, nq - 1, 0)).astype(BF)
    q_ref[2] = jnp.where(colq == 0, 0.0, pltpu.roll(y, 1, 0)).astype(BF)

    def back(r0, rows):
        acc = jnp.zeros((rows, C), F32)
        for a in range(3):
            for b in range(3):
                first = (2 - a) * TS + r0
                acc = acc + lax.dot_general(q_ref[b, first : first + rows, :], w_ref[a, b], NT, preferred_element_type=F32)
        return acc

    rid = lax.broadcasted_iota(I32, (TS, C), 0)
    sides = []
    for c, b in ((0, 0), (TS - 1, 2)):
        e = gf_ref[...].reshape(TS, TS, C)[:, c, :]
        up = jnp.where(rid == TS - 1, 0.0, pltpu.roll(e, TS - 1, 0))
        down = jnp.where(rid == 0, 0.0, pltpu.roll(e, 1, 0))
        acc = jnp.zeros((TS, C), F32)
        for a, v in ((0, up), (1, e), (2, down)):
            acc = acc + lax.dot_general(v.astype(BF), w_ref[a, b], NT, preferred_element_type=F32)
        sides.append(acc)
    split_lines(flags, back(0, TS), back(33 * TS, TS), sides[0], sides[1], inner_ref, outer_ref)
    for m in range(PIX // step):
        mid_ref[m * step : (m + 1) * step, :] = back(TS + m * step, step)


def conv(flags, field, inner, near, far, w, bias, cot):
    return pl.pallas_call(
        conv_kernel,
        out_shape=[
            jax.ShapeDtypeStruct((PIX, C), BF),
            jax.ShapeDtypeStruct((PIX, C), BF),
            jax.ShapeDtypeStruct((3, 34 * TS, C), BF),
            jax.ShapeDtypeStruct((PIX, C), F32),
        ] + LINES,
        in_specs=[SM, VM, VM, HB, HB, VM, VM, VM],
        out_specs=[VM] * 6,
        scratch_shapes=[pltpu.VMEM((3, 36 * TS, C), BF), pltpu.VMEM((PIX, C), F32)] + EDGE_SCRATCH,
        compiler_params=params(40),
        cost_estimate=cost(9 * 2**29 * 3, 2**23),
    )(flags, field, inner, near, far, w, bias, cot)


def tap_kernel(p_ref, gp_ref, wg_ref, bg_ref):
    turned = gp_ref[...].T
    for a in range(3):
        for b in range(3):
            wg_ref[a, b] = jnp.dot(turned, p_ref[b, a * TS : a * TS + PIX, :], preferred_element_type=F32).T
    bg_ref[...] = jnp.sum(gp_ref[...].astype(F32), axis=0, keepdims=True)


def tap_grads(p, gp):
    return pl.pallas_call(
        tap_kernel,
        out_shape=(jax.ShapeDtypeStruct((3, 3, C, C), F32), jax.ShapeDtypeStruct((1, C), F32)),
        in_specs=[VM] * 2,
        out_specs=[VM] * 2,
        compiler_params=params(24),
        cost_estimate=cost(9 * 2**27 * 4, 2**22),
    )(p, gp)


def total_kernel(flags, mid_ref, in_ref, near_ref, far_ref, out_ref, buf_ref, sem):
    outer_copies(flags, near_ref, far_ref, buf_ref, sem)
    north, south, west, east = join_lines(flags, in_ref, buf_ref)
    col = lax.broadcasted_iota(I32, (PIX, C), 0) % TS
    x = mid_ref[...]
    x = x + jnp.where(col == 0, spread_rows(west), 0.0) + jnp.where(col == TS - 1, spread_rows(east), 0.0)
    out_ref[...] = x.astype(BF)
    out_ref[0:TS, :] = (x[0:TS] + north).astype(BF)
    out_ref[PIX - TS : PIX, :] = (x[PIX - TS : PIX] + south).astype(BF)


def field_grad(flags, mid, inner, near, far):
    return pl.pallas_call(
        total_kernel,
        out_shape=jax.ShapeDtypeStruct((PIX, C), BF),
        in_specs=[SM, VM, VM, HB, HB],
        out_specs=VM,
        scratch_shapes=EDGE_SCRATCH,
        compiler_params=params(24),
        cost_estimate=cost(2**20, 2**21),
    )(flags, mid, inner, near, far)


def shards(latlon, send_rows, send_count, interp_slot, interp_weight, outer_partner, outer_side, outer_flip,
           conv_weight, conv_bias, cotangent):
    faces = lax.axis_size("face")
    face = lax.axis_index("face")
    j = lax.axis_index("tile")
    steps = jnp.arange(4, dtype=I32)
    owner = (j + steps) % 4
    group = jnp.concatenate([4 + j - owner, (j - owner) % 8])

    mine = jnp.concatenate([interp_slot.T.astype(F32), interp_weight.T])
    asked = [mine] + [along_tile(mine, -k) for k in (1, 2, 3)]
    asked = jnp.stack(asked + [from_far_tile(mine, k, faces) for k in range(4)])
    first = jnp.concatenate([jnp.broadcast_to((group * CAP).astype(F32)[:, None], (8, 4)), jnp.zeros((8, 4), F32)], axis=1)
    meta = asked - first[:, :, None]
    meta_cols = meta.transpose(0, 2, 1)
    live = jnp.arange(CAP, dtype=I32)[None, :] < send_count[0][:, None]
    idx = jnp.where(live, send_rows[0], -1)[group]
    idx_cols = idx.T

    partner = outer_partner[0, 0]
    away = partner ^ face
    place = (((face >> 3) - (partner >> 3)) & 3) * 4 + (((face >> 1) - (partner >> 1)) & 3)
    corner = jnp.stack([(j // 2 == 0), (j % 2 == 0)]).astype(I32)
    flags = jnp.concatenate([place, outer_side[0, 0], outer_flip[0, 0], corner, away & 1]).astype(I32)

    far = []
    for pair in (0, 2):
        part = partial_sums(idx_cols[:, 4 + pair : 6 + pair], meta_cols[4 + pair : 6 + pair], latlon)
        far += [to_far(part[i], pair + i, faces) for i in range(2)]
    near = []
    part = partial_sums(idx_cols[:, 1:3], meta_cols[1:3], latlon, jnp.stack(far[1:3]))
    moved = [along_tile(part[0], 1), along_tile(part[1], 2)]
    part = partial_sums(idx_cols[:, 3:4], meta_cols[3:4], latlon, far[3][None])
    moved.append(along_tile(part[0], 3))
    part = partial_sums(idx_cols[:, 0:1], meta_cols[0:1], latlon, far[0][None])
    field, inner, outer = make_field(flags, [part[0]] + moved)
    inner, plane, twin = exchange(inner, outer)
    activated, grad_pre, windows, mid, inner, outer = conv(
        flags, field, inner, plane, twin, conv_weight, conv_bias[None, :], cotangent
    )
    inner, plane, twin = exchange(inner, outer)
    weight_part, bias_part = tap_grads(windows, grad_pre)
    grad_weight, grad_bias = lax.psum((weight_part, bias_part[0]), AXES)
    whole = field_grad(flags, mid, inner, plane, twin)
    near = [whole] + [along_tile(whole, -k) for k in (1, 2, 3)]
    far = [from_far(near[k], k, faces) for k in range(4)]
    rows = row_grads(idx[0:4], meta[0:4], near, None, F32)
    grad_latlon = row_grads(idx[4:8], meta[4:8], far, rows, BF)
    return activated, grad_latlon, grad_weight, grad_bias


def solution(mesh):
    both = ("face", "tile")
    placed = (
        P(both, None), P(both, None, None), P(both, None), P(both, None), P(both, None),
        P("face", "tile", None), P("face", "tile", None), P("face", "tile", None), P(), P(), P(both, None),
    )
    return jax.shard_map(
        shards, mesh=mesh, in_specs=placed, out_specs=(P(both, None), P(both, None), P(), P()), check_vma=False
    )
```

```python
import functools
import jax
import jax.numpy as jnp
from jax import lax
from jax.experimental import pallas as pl
from jax.experimental.pallas import tpu as pltpu
from jax.sharding import PartitionSpec as P

BF = jnp.bfloat16
F32 = jnp.float32
I16 = jnp.int16
I32 = jnp.int32
AXES = ("face", "tile")
TS = 32
PIX = 1024
CAP = 1024
ROWS = 4096
C = 256
MT = 512
KC = 256

root_half = 0.7071067811865476
inv_root_two_pi = 0.3989422804014327
VM = pl.BlockSpec(memory_space=pltpu.VMEM)
SM = pl.BlockSpec(memory_space=pltpu.SMEM)
HB = pl.BlockSpec(memory_space=pl.ANY)
NT = (((1,), (1,)), ((), ()))


def params(mib):
    return pltpu.CompilerParams(vmem_limit_bytes=mib * 2**20)


def cost(flops, size):
    return pl.CostEstimate(flops=flops, bytes_accessed=size, transcendentals=0)


def far_face(j, k):
    return 1 if k == 0 or j + k >= 4 else -1


def to_far(value, k, faces):
    pairs = []
    for face in range(faces):
        for j in range(4):
            pairs.append((face * 4 + j, (face + far_face(j, k)) % faces * 4 + j))
    return lax.ppermute(value, AXES, pairs)


def from_far(value, k, faces):
    pairs = []
    for face in range(faces):
        for j in range(4):
            pairs.append(((face + far_face(j, k)) % faces * 4 + j, face * 4 + j))
    return lax.ppermute(value, AXES, pairs)


def from_far_tile(value, k, faces):
    pairs = []
    for face in range(faces):
        for j in range(4):
            pairs.append(((face + far_face(j, k)) % faces * 4 + (j + k) % 4, face * 4 + j))
    return lax.ppermute(value, AXES, pairs)


def along_tile(value, k):
    return lax.ppermute(value, "tile", [(i, (i + k) % 4) for i in range(4)])


def along_x(value, k):
    return lax.ppermute(value, "face", [(i, (i & ~6) | ((((i >> 1) + k) & 3) << 1)) for i in range(32)])


def along_z(value, k):
    return lax.ppermute(value, "face", [(i, (i + 8 * k) % 32) for i in range(32)])


def other_core(value):
    return lax.ppermute(value, "face", [(i, i ^ 1) for i in range(32)])


def lanes_iota(shape, dim, dtype):
    return lax.broadcasted_iota(I32, shape, dim).astype(dtype)


def gather_kernel(picks, idx_ref, table_ref, *outs):
    base = lanes_iota((MT, KC), 1, I16)
    one = jnp.ones((MT, KC), BF)
    zero = jnp.zeros((MT, KC), BF)
    for b, out_ref in zip(picks, outs):
        def pick(m, carry):
            rows = pl.ds(pl.multiple_of(m * MT, MT), MT)
            wide = jnp.broadcast_to(idx_ref[rows, b : b + 1], (MT, 128)).astype(I16)
            want = jnp.concatenate([wide] * (KC // 128), axis=1)
            acc = jnp.zeros((MT, C), F32)
            for k in range(ROWS // KC):
                hot = jnp.where(want == base + jnp.asarray(k * KC, I16), one, zero)
                acc = acc + jnp.dot(hot, table_ref[k * KC : (k + 1) * KC, :], preferred_element_type=F32)
            out_ref[rows, :] = acc.astype(BF)
            return carry

        lax.fori_loop(0, CAP // MT, pick, 0)


def gather_rows(picks, idx, table):
    n = len(picks)
    return pl.pallas_call(
        functools.partial(gather_kernel, picks),
        out_shape=[jax.ShapeDtypeStruct((CAP, C), BF)] * n,
        in_specs=[VM] * 2,
        out_specs=[VM] * n,
        compiler_params=params(24),
        cost_estimate=cost(n * 2**31 * 2, 2**21),
    )(idx, table)


def mix_kernel(which, spans, flags, ask_ref, got_ref, *rest):
    adds = rest[:-1]
    out_ref = rest[-1]
    base = lanes_iota((MT, KC), 1, I16)
    zero = jnp.zeros((MT, KC), BF)
    first = (flags[10 + which] * CAP).astype(F32)
    row = lax.broadcasted_iota(I32, (8, PIX), 0)
    ask = jnp.where(row < 4, ask_ref[...] - first, ask_ref[...]).T

    def spread(col, dtype):
        wide = jnp.broadcast_to(col, (MT, 128))
        wide = wide.astype(I32).astype(I16) if dtype == I16 else wide.astype(dtype)
        return jnp.concatenate([wide] * (KC // 128), axis=1)

    for m in range(PIX // MT):
        rows = slice(m * MT, (m + 1) * MT)
        slots = [spread(ask[rows, k : k + 1], I16) for k in range(4)]
        scale = [spread(ask[rows, 4 + k : 5 + k], BF) for k in range(4)]
        acc = jnp.zeros((MT, C), F32)
        for ref, (lo, hi) in zip(adds, spans):
            if lo <= m * MT and (m + 1) * MT <= hi:
                acc = acc + ref[m * MT - lo : (m + 1) * MT - lo, :].astype(F32)
        for q in range(CAP // KC):
            here = base + jnp.asarray(q * KC, I16)
            w = jnp.where(slots[0] == here, scale[0], zero)
            for k in range(1, 4):
                w = w + jnp.where(slots[k] == here, scale[k], zero)
            acc = acc + jnp.dot(w, got_ref[q * KC : (q + 1) * KC, :], preferred_element_type=F32)
        out_ref[rows, :] = acc.astype(BF)


def mix(flags, which, ask, got, adds=()):
    spans = [(lo, lo + value.shape[0]) for value, lo in adds]
    extra = [value for value, lo in adds]
    return pl.pallas_call(
        functools.partial(mix_kernel, which, spans),
        out_shape=jax.ShapeDtypeStruct((PIX, C), BF),
        in_specs=[SM] + [VM] * (2 + len(extra)),
        out_specs=VM,
        compiler_params=params(24),
        cost_estimate=cost(2**29 * 2, 2**21),
    )(flags, ask, got, *extra)


PUT = 1024


def scatter_kernel(blocks, halves, has_add, flags, idx_ref, *rest):
    n = len(blocks)
    asks = rest[:n]
    rest = rest[n:]
    grads = []
    for h in halves:
        grads.append(rest[:h])
        rest = rest[h:]
    if has_add:
        add_ref, out_ref, slot_ref = rest
    else:
        out_ref, slot_ref = rest

    def spread(row, rows, dtype):
        tall = jnp.broadcast_to(row, (16, KC)).astype(dtype)
        return jnp.broadcast_to(tall[None], (rows // 16, 16, KC)).reshape(rows, KC)

    @pl.when(pl.program_id(0) == 0)
    def _():
        base = lanes_iota((MT, KC), 0, I16)
        zero = jnp.zeros((MT, KC), BF)
        for i in range(n):
            group = (flags[10 + blocks[i]] * CAP).astype(F32)

            def mixed(m, carry):
                first = group + (m * MT).astype(F32)
                acc = jnp.zeros((MT, C), F32)
                for q in range(PIX // KC):
                    lanes = slice(q * KC, (q + 1) * KC)
                    w = None
                    for k in range(4):
                        slots = spread((asks[i][k : k + 1, lanes] - first).astype(I32), MT, I16)
                        term = jnp.where(slots == base, spread(asks[i][4 + k : 5 + k, lanes], MT, BF), zero)
                        w = term if w is None else w + term
                    part = PIX // halves[i]
                    ref = grads[i][q * KC // part]
                    at = q * KC % part
                    acc = acc + jnp.dot(w, ref[at : at + KC, :], preferred_element_type=F32)
                slot_ref[pl.ds(pl.multiple_of(i * CAP + m * MT, MT), MT), :] = acc.astype(BF)
                return carry

            lax.fori_loop(0, CAP // MT, mixed, 0)

    base = lanes_iota((PUT, KC), 0, I16)
    one = jnp.ones((PUT, KC), BF)
    zero = jnp.zeros((PUT, KC), BF)
    first = pl.program_id(0) * PUT
    acc = add_ref[...] if has_add else jnp.zeros((PUT, C), F32)
    for i in range(n):
        for q in range(CAP // KC):
            want = spread(idx_ref[blocks[i] : blocks[i] + 1, q * KC : (q + 1) * KC] - first, PUT, I16)
            hot = jnp.where(want == base, one, zero)
            at = i * CAP + q * KC
            acc = acc + jnp.dot(hot, slot_ref[at : at + KC, :], preferred_element_type=F32)
    out_ref[...] = acc.astype(out_ref.dtype)


def row_grads(flags, idx, blocks, asks, grads, add, dtype):
    n = len(blocks)
    has_add = add is not None
    grads = [g if isinstance(g, tuple) else (g,) for g in grads]
    halves = [len(g) for g in grads]
    whole = [idx, *asks] + [x for g in grads for x in g]
    tile = pl.BlockSpec((PUT, C), lambda m: (m, 0))
    specs = [SM] + [pl.BlockSpec(x.shape, lambda m: (0, 0)) for x in whole] + ([tile] if has_add else [])
    return pl.pallas_call(
        functools.partial(scatter_kernel, blocks, halves, has_add),
        grid=(ROWS // PUT,),
        out_shape=jax.ShapeDtypeStruct((ROWS, C), dtype),
        in_specs=specs,
        out_specs=tile,
        scratch_shapes=[pltpu.VMEM((n * CAP, C), BF)],
        compiler_params=params(40),
        cost_estimate=cost(n * 2**31 * 2, 2**22),
    )(flags, *whole, *([add] if has_add else []))


def spread_rows(lines):
    rows = lines.shape[0]
    return jnp.broadcast_to(lines[:, None, :], (rows, TS, C)).reshape(rows * TS, C)


def split_lines(flags, north, south, west, east, inner_ref, outer_ref):
    top = flags[6] == 1
    left = flags[7] == 1
    inner_ref[0] = jnp.where(top, south, north).astype(BF)
    inner_ref[1] = jnp.where(left, east, west).astype(BF)
    outer_ref[0] = jnp.where(top, north, south).astype(BF)
    outer_ref[1] = jnp.where(left, west, east).astype(BF)


def outer_copies(flags, near_ref, far_ref, buf_ref, sem):
    for s in range(2):
        @pl.when(flags[8 + s] == 0)
        def _():
            pltpu.make_async_copy(near_ref.at[flags[s], flags[2 + s]], buf_ref.at[s], sem.at[s]).start()

        @pl.when(flags[8 + s] != 0)
        def _():
            pltpu.make_async_copy(far_ref.at[flags[s], flags[2 + s]], buf_ref.at[s], sem.at[s]).start()
    for s in range(2):
        pltpu.make_async_copy(near_ref.at[0, 0], buf_ref.at[s], sem.at[s]).wait()


def join_lines(flags, inner_ref, buf_ref):
    row = lax.broadcasted_iota(I32, (TS, TS), 0)
    col = lax.broadcasted_iota(I32, (TS, TS), 1)
    turn = (row + col == TS - 1).astype(BF)
    outer = []
    for s in range(2):
        line = buf_ref[s]
        back = jnp.dot(turn, line, preferred_element_type=F32)
        outer.append(jnp.where(flags[4 + s] == 1, back, line.astype(F32)))
    top = flags[6] == 1
    left = flags[7] == 1
    in_rows = inner_ref[0].astype(F32)
    in_cols = inner_ref[1].astype(F32)
    north = jnp.where(top, outer[0], in_rows)
    south = jnp.where(top, in_rows, outer[0])
    west = jnp.where(left, outer[1], in_cols)
    east = jnp.where(left, in_cols, outer[1])
    return north, south, west, east


def exchange(inner, outer):
    rows = lax.ppermute(inner[0], "tile", [(i, i ^ 2) for i in range(4)])
    cols = lax.ppermute(inner[1], "tile", [(i, i ^ 1) for i in range(4)])
    line = jnp.stack([outer] + [along_x(outer, k) for k in (1, 2, 3)])
    plane = jnp.concatenate([line] + [along_z(line, k) for k in (1, 2, 3)])
    return jnp.stack([rows, cols]), plane, other_core(plane)


EDGE_SCRATCH = [pltpu.VMEM((2, TS, C), BF), pltpu.SemaphoreType.DMA((2,))]
LINES = [jax.ShapeDtypeStruct((2, TS, C), BF)] * 2


def field_kernel(flags, a_ref, b_ref, c_ref, field_ref, inner_ref, outer_ref):
    total = a_ref[...].astype(F32) + b_ref[...].astype(F32) + c_ref[...].astype(F32)
    field_ref[...] = total.astype(BF)
    grid = total.reshape(TS, TS, C)
    split_lines(flags, total[0:TS], total[PIX - TS : PIX], grid[:, 0, :], grid[:, TS - 1, :], inner_ref, outer_ref)


def make_field(flags, parts):
    return pl.pallas_call(
        field_kernel,
        out_shape=[jax.ShapeDtypeStruct((PIX, C), BF)] + LINES,
        in_specs=[SM] + [VM] * 3,
        out_specs=[VM] * 3,
        compiler_params=params(24),
        cost_estimate=cost(2**20, 3 * 2**20),
    )(flags, *parts)


def conv_kernel(flags, field_ref, in_ref, near_ref, far_ref, w_ref, bias_ref, cot_ref,
                act_ref, gp_ref, p_ref, mid_ref, inner_ref, outer_ref, q_ref, gf_ref, buf_ref, sem):
    n = 34 * TS
    outer_copies(flags, near_ref, far_ref, buf_ref, sem)
    north, south, west, east = join_lines(flags, in_ref, buf_ref)
    zero = jnp.zeros((1, C), F32)
    p_ref[1, 0:TS, :] = north.astype(BF)
    p_ref[1, TS : TS + PIX, :] = field_ref[...]
    p_ref[1, TS + PIX : n, :] = south.astype(BF)
    x = p_ref[1].astype(F32)
    col = lax.broadcasted_iota(I32, (n, C), 0) % TS
    west = jnp.concatenate([zero, west, zero])
    east = jnp.concatenate([zero, east, zero])
    p_ref[0] = jnp.where(col == 0, spread_rows(west), pltpu.roll(x, 1, 0)).astype(BF)
    p_ref[2] = jnp.where(col == TS - 1, spread_rows(east), pltpu.roll(x, n - 1, 0)).astype(BF)
    step = 256
    q_ref[1, 0 : 2 * TS, :] = jnp.zeros((2 * TS, C), BF)
    q_ref[1, 2 * TS + PIX : 4 * TS + PIX, :] = jnp.zeros((2 * TS, C), BF)
    for m in range(PIX // step):
        rows = slice(m * step, (m + 1) * step)
        pre = jnp.broadcast_to(bias_ref[...], (step, C))
        for a in range(3):
            for b in range(3):
                pre = pre + jnp.dot(
                    p_ref[b, a * TS + m * step : a * TS + (m + 1) * step, :], w_ref[a, b], preferred_element_type=F32
                )
        cdf = 0.5 * (1.0 + lax.erf(pre * root_half))
        act_ref[rows, :] = (pre * cdf).astype(BF)
        slope = cdf + pre * inv_root_two_pi * jnp.exp(-0.5 * pre * pre)
        g = (cot_ref[rows, :].astype(F32) * slope).astype(BF)
        gp_ref[rows, :] = g
        q_ref[1, 2 * TS + m * step : 2 * TS + (m + 1) * step, :] = g
        gf_ref[rows, :] = g.astype(F32)
    nq = 36 * TS
    y = q_ref[1].astype(F32)
    colq = lax.broadcasted_iota(I32, (nq, C), 0) % TS
    q_ref[0] = jnp.where(colq == TS - 1, 0.0, pltpu.roll(y, nq - 1, 0)).astype(BF)
    q_ref[2] = jnp.where(colq == 0, 0.0, pltpu.roll(y, 1, 0)).astype(BF)

    def back(r0, rows):
        acc = jnp.zeros((rows, C), F32)
        for a in range(3):
            for b in range(3):
                first = (2 - a) * TS + r0
                acc = acc + lax.dot_general(q_ref[b, first : first + rows, :], w_ref[a, b], NT, preferred_element_type=F32)
        return acc

    rid = lax.broadcasted_iota(I32, (TS, C), 0)
    sides = []
    for c, b in ((0, 0), (TS - 1, 2)):
        e = gf_ref[...].reshape(TS, TS, C)[:, c, :]
        up = jnp.where(rid == TS - 1, 0.0, pltpu.roll(e, TS - 1, 0))
        down = jnp.where(rid == 0, 0.0, pltpu.roll(e, 1, 0))
        acc = jnp.zeros((TS, C), F32)
        for a, v in ((0, up), (1, e), (2, down)):
            acc = acc + lax.dot_general(v.astype(BF), w_ref[a, b], NT, preferred_element_type=F32)
        sides.append(acc)
    split_lines(flags, back(0, TS), back(33 * TS, TS), sides[0], sides[1], inner_ref, outer_ref)
    for m in range(PIX // step):
        mid_ref[m * step : (m + 1) * step, :] = back(TS + m * step, step)


def conv(flags, field, inner, near, far, w, bias, cot):
    return pl.pallas_call(
        conv_kernel,
        out_shape=[
            jax.ShapeDtypeStruct((PIX, C), BF),
            jax.ShapeDtypeStruct((PIX, C), BF),
            jax.ShapeDtypeStruct((3, 34 * TS, C), BF),
            jax.ShapeDtypeStruct((PIX, C), F32),
        ] + LINES,
        in_specs=[SM, VM, VM, HB, HB, VM, VM, VM],
        out_specs=[VM] * 6,
        scratch_shapes=[pltpu.VMEM((3, 36 * TS, C), BF), pltpu.VMEM((PIX, C), F32)] + EDGE_SCRATCH,
        compiler_params=params(40),
        cost_estimate=cost(9 * 2**29 * 3, 2**23),
    )(flags, field, inner, near, far, w, bias, cot)


TAPS = 9 * C
PADDED = 2560


def tap_kernel(p_ref, gp_ref, out_ref):
    turned = gp_ref[...].T
    for a in range(3):
        for b in range(3):
            at = (a * 3 + b) * C
            part = jnp.dot(turned, p_ref[b, a * TS : a * TS + PIX, :], preferred_element_type=F32)
            out_ref[at : at + C, :] = part.T.astype(BF)
    bias = jnp.sum(gp_ref[...].astype(F32), axis=0, keepdims=True)
    row = lax.broadcasted_iota(I32, (PADDED - TAPS, C), 0)
    out_ref[TAPS:PADDED, :] = jnp.where(row == 0, bias, 0.0).astype(BF)


def tap_grads(p, gp):
    return pl.pallas_call(
        tap_kernel,
        out_shape=jax.ShapeDtypeStruct((PADDED, C), BF),
        in_specs=[VM] * 2,
        out_specs=VM,
        compiler_params=params(24),
        cost_estimate=cost(9 * 2**27 * 4, 2**22),
    )(p, gp)


def summed(parts):
    total = parts[0].astype(F32)
    for part in parts[1:]:
        total = total + part.astype(F32)
    return total.astype(BF)


def reduce_pieces(value, place, move):
    size = value.shape[0] // 4
    parts = [lax.dynamic_slice_in_dim(value, ((place + k) & 3) * size, size, 0) for k in range(4)]
    return summed([parts[0]] + [move(parts[k], k) for k in (1, 2, 3)])


def sum_taps(value, face, j):
    half = PADDED // 2
    core = face & 1
    kept = lax.dynamic_slice_in_dim(value, core * half, half, 0)
    given = lax.dynamic_slice_in_dim(value, (1 - core) * half, half, 0)
    value = summed([kept, other_core(given)])
    value = reduce_pieces(value, j, along_tile)
    x = (face >> 1) & 3
    value = reduce_pieces(value, x, along_x)
    value = summed([value] + [along_z(value, k) for k in (1, 2, 3)])
    line = jnp.stack([value] + [along_x(value, k) for k in (1, 2, 3)])
    value = line[(x - jnp.arange(4, dtype=I32)) & 3].reshape(4 * value.shape[0], C)
    mine = jnp.stack([value] + [along_tile(value, k) for k in (1, 2, 3)])
    return mine, other_core(mine)


def place_kernel(flags, mine_ref, other_ref, taps_ref, bias_ref, all_ref):
    size = PADDED // 8
    core = flags[18]
    j = flags[19]
    for k in range(4):
        at = lax.rem(j + 4 - k, 4) * size
        lo = pl.multiple_of(core * (PADDED // 2) + at, 64)
        hi = pl.multiple_of((1 - core) * (PADDED // 2) + at, 64)
        all_ref[pl.ds(lo, size), :] = mine_ref[k].astype(F32)
        all_ref[pl.ds(hi, size), :] = other_ref[k].astype(F32)
    taps_ref[...] = all_ref[0:TAPS, :]
    bias_ref[...] = all_ref[TAPS : TAPS + 1, :]


def place_taps(flags, mine, other):
    taps, bias = pl.pallas_call(
        place_kernel,
        out_shape=(jax.ShapeDtypeStruct((TAPS, C), F32), jax.ShapeDtypeStruct((1, C), F32)),
        in_specs=[SM, VM, VM],
        out_specs=[VM, VM],
        scratch_shapes=[pltpu.VMEM((PADDED, C), F32)],
        compiler_params=params(24),
        cost_estimate=cost(2**20, 2**22),
    )(flags, mine, other)
    return taps.reshape(3, 3, C, C), bias[0]


def total_kernel(flags, mid_ref, in_ref, near_ref, far_ref, out_ref, buf_ref, sem):
    outer_copies(flags, near_ref, far_ref, buf_ref, sem)
    north, south, west, east = join_lines(flags, in_ref, buf_ref)
    col = lax.broadcasted_iota(I32, (PIX, C), 0) % TS
    x = mid_ref[...]
    x = x + jnp.where(col == 0, spread_rows(west), 0.0) + jnp.where(col == TS - 1, spread_rows(east), 0.0)
    out_ref[...] = x.astype(BF)
    out_ref[0:TS, :] = (x[0:TS] + north).astype(BF)
    out_ref[PIX - TS : PIX, :] = (x[PIX - TS : PIX] + south).astype(BF)


def field_grad(flags, mid, inner, near, far):
    return pl.pallas_call(
        total_kernel,
        out_shape=jax.ShapeDtypeStruct((PIX, C), BF),
        in_specs=[SM, VM, VM, HB, HB],
        out_specs=VM,
        scratch_shapes=EDGE_SCRATCH,
        compiler_params=params(24),
        cost_estimate=cost(2**20, 2**21),
    )(flags, mid, inner, near, far)


def shards(latlon, send_rows, send_count, interp_slot, interp_weight, outer_partner, outer_side, outer_flip,
           conv_weight, conv_bias, cotangent):
    faces = lax.axis_size("face")
    face = lax.axis_index("face")
    j = lax.axis_index("tile")
    steps = jnp.arange(4, dtype=I32)
    owner = (j + steps) % 4
    group = jnp.concatenate([4 + j - owner, (j - owner) % 8])

    mine = jnp.concatenate([interp_slot.T.astype(F32), interp_weight.T])
    ask = [mine] + [along_tile(mine, -k) for k in (1, 2, 3)] + [from_far_tile(mine, k, faces) for k in range(4)]
    live = jnp.arange(CAP, dtype=I32)[None, :] < send_count[0][:, None]
    idx = jnp.where(live, send_rows[0], -1)[group]
    idx_cols = idx.T

    partner = outer_partner[0, 0]
    away = partner ^ face
    place = (((face >> 3) - (partner >> 3)) & 3) * 4 + (((face >> 1) - (partner >> 1)) & 3)
    corner = jnp.stack([(j // 2 == 0), (j % 2 == 0)]).astype(I32)
    here = jnp.stack([face & 1, j])
    flags = jnp.concatenate([place, outer_side[0, 0], outer_flip[0, 0], corner, away & 1, group, here]).astype(I32)

    got = {}
    for pair in ((4, 6), (5, 7), (2, 1), (3, 0)):
        got.update(zip(pair, gather_rows(pair, idx_cols, latlon)))
    far = [None] * 4
    for k in (0, 2, 1, 3):
        far[k] = to_far(mix(flags, 4 + k, ask[4 + k], got[4 + k]), k, faces)
    part = mix(flags, 2, ask[2], got[2], [(far[2], 0)])
    low = along_tile(part[: PIX // 2], 1)
    high = along_tile(part[PIX // 2 :], -1)
    moved = [along_tile(mix(flags, 1, ask[1], got[1], [(far[1], 0), (low, 0)]), 1)]
    moved.append(along_tile(mix(flags, 3, ask[3], got[3], [(far[3], 0), (high, PIX // 2)]), -1))
    part = mix(flags, 0, ask[0], got[0], [(far[0], 0)])
    field, inner, outer = make_field(flags, [part] + moved)
    inner, plane, twin = exchange(inner, outer)
    activated, grad_pre, windows, mid, inner, outer = conv(
        flags, field, inner, plane, twin, conv_weight, conv_bias[None, :], cotangent
    )
    inner, plane, twin = exchange(inner, outer)
    taps = sum_taps(tap_grads(windows, grad_pre), face, j)
    whole = field_grad(flags, mid, inner, plane, twin)
    up = along_tile(whole, -1)
    down = along_tile(whole, 1)
    across = (along_tile(up[: PIX // 2], -1), along_tile(down[PIX // 2 :], 1))
    far = [from_far(whole, 0, faces), from_far(up, 1, faces), None, from_far(down, 3, faces)]
    far[2] = tuple(from_far(part, 2, faces) for part in across)
    rows = row_grads(flags, idx, (0, 4), (ask[0], ask[4]), (whole, far[0]), None, F32)
    rows = row_grads(flags, idx, (1, 3), (ask[1], ask[3]), (up, down), rows, F32)
    rows = row_grads(flags, idx, (5, 7), (ask[5], ask[7]), (far[1], far[3]), rows, F32)
    grad_latlon = row_grads(flags, idx, (2, 6), (ask[2], ask[6]), (across, far[2]), rows, BF)
    grad_weight, grad_bias = place_taps(flags, *taps)
    return activated, grad_latlon, grad_weight, grad_bias


def solution(mesh):
    both = ("face", "tile")
    placed = (
        P(both, None), P(both, None, None), P(both, None), P(both, None), P(both, None),
        P("face", "tile", None), P("face", "tile", None), P("face", "tile", None), P(), P(), P(both, None),
    )
    return jax.shard_map(
        shards, mesh=mesh, in_specs=placed, out_specs=(P(both, None), P(both, None), P(), P()), check_vma=False
    )
```

```python
import functools
import jax
import jax.numpy as jnp
from jax import lax
from jax.experimental import pallas as pl
from jax.experimental.pallas import tpu as pltpu
from jax.sharding import PartitionSpec as P

BF = jnp.bfloat16
F32 = jnp.float32
I16 = jnp.int16
I32 = jnp.int32
AXES = ("face", "tile")
TS = 32
PIX = 1024
CAP = 1024
ROWS = 4096
C = 256
MT = 512
KC = 256

FACE, TILE, FLIP, TOP, LEFT, GROUP, WHOSE = 0, 1, 2, 4, 5, 6, 14

root_half = 0.7071067811865476
inv_root_two_pi = 0.3989422804014327
VM = pl.BlockSpec(memory_space=pltpu.VMEM)
SM = pl.BlockSpec(memory_space=pltpu.SMEM)
HB = pl.BlockSpec(memory_space=pl.ANY)
NT = (((1,), (1,)), ((), ()))


def params(mib):
    return pltpu.CompilerParams(vmem_limit_bytes=mib * 2**20)


def cost(flops, size):
    return pl.CostEstimate(flops=flops, bytes_accessed=size, transcendentals=0)


def far_face(j, k):
    return 1 if j ^ k <= j else -1


def to_far(value, k, faces):
    pairs = []
    for face in range(faces):
        for j in range(4):
            pairs.append((face * 4 + j, (face + far_face(j, k)) % faces * 4 + j))
    return lax.ppermute(value, AXES, pairs)


def from_far(value, k, faces):
    pairs = []
    for face in range(faces):
        for j in range(4):
            pairs.append(((face + far_face(j, k)) % faces * 4 + j, face * 4 + j))
    return lax.ppermute(value, AXES, pairs)


def from_face(value, step, faces):
    return lax.ppermute(value, "face", [((i + step) % faces, i) for i in range(faces)])


def along_tile(value, k):
    return lax.ppermute(value, "tile", [(i, i ^ k) for i in range(4)])


def first_step(i):
    return 2 if i & 1 else 8


def second_step(i):
    return 8 if i & 1 else 2


def along_first(value, k):
    return lax.ppermute(value, "face", [(i, i ^ (k * first_step(i))) for i in range(32)])


def along_second(value, k):
    return lax.ppermute(value, "face", [(i, i ^ (k * second_step(i))) for i in range(32)])


def other_core(value):
    return lax.ppermute(value, "face", [(i, i ^ 1) for i in range(32)])


def gate(value, after):
    return lax.optimization_barrier((value, after))


def lanes_iota(shape, dim, dtype):
    return lax.broadcasted_iota(I32, shape, dim).astype(dtype)


def pick_rows(want, table_ref):
    base = lanes_iota((MT, KC), 1, I16)
    one = jnp.ones((MT, KC), BF)
    zero = jnp.zeros((MT, KC), BF)
    want = jnp.concatenate([jnp.broadcast_to(want, (MT, 128)).astype(I16)] * (KC // 128), axis=1)
    acc = jnp.zeros((MT, C), F32)
    for k in range(ROWS // KC):
        hot = jnp.where(want == base + jnp.asarray(k * KC, I16), one, zero)
        acc = acc + jnp.dot(hot, table_ref[k * KC : (k + 1) * KC, :], preferred_element_type=F32)
    return acc.astype(BF)


SUB = 64


def weigh(first, ask, w_ref):
    base = lanes_iota((SUB, 128), 1, I16)
    zero = jnp.zeros((SUB, 128), BF)
    row = lax.broadcasted_iota(I32, (8, PIX), 0)
    ask = jnp.where(row < 4, ask - first, ask).T
    for p in range(0, PIX, SUB):
        slots = [jnp.broadcast_to(ask[p : p + SUB, k : k + 1], (SUB, 128)).astype(I32).astype(I16) for k in range(4)]
        scale = [jnp.broadcast_to(ask[p : p + SUB, 4 + k : 5 + k], (SUB, 128)).astype(BF) for k in range(4)]
        for q in range(0, CAP, 128):
            here = base + jnp.asarray(q, I16)
            w = jnp.where(slots[0] == here, scale[0], zero)
            for k in range(1, 4):
                w = w + jnp.where(slots[k] == here, scale[k], zero)
            w_ref[p : p + SUB, q : q + 128] = w


def sum_kernel(which, has_add, flags, idx_ref, table_ref, ask_ref, *rest):
    if has_add:
        out_ref, done_ref, got_ref, w_ref, add_ref, sem = rest[-6:]
        copy = pltpu.make_async_copy(rest[0], add_ref, sem)
        copy.start()
    else:
        out_ref, done_ref, got_ref, w_ref = rest[-4:]
    done_ref[...] = jnp.zeros_like(done_ref)
    weigh((flags[GROUP + which] * CAP).astype(F32), ask_ref[flags[WHOSE + which]], w_ref)
    for m in range(0, CAP, MT):
        got_ref[m : m + MT, :] = pick_rows(idx_ref[m : m + MT, which : which + 1], table_ref)
    if has_add:
        copy.wait()
    for m in range(0, PIX, MT):
        acc = add_ref[m : m + MT, :].astype(F32) if has_add else jnp.zeros((MT, C), F32)
        for q in range(0, CAP, KC):
            acc = acc + jnp.dot(w_ref[m : m + MT, q : q + KC], got_ref[q : q + KC, :], preferred_element_type=F32)
        out_ref[m : m + MT, :] = acc.astype(BF)


def partial_sum(flags, which, idx, table, ask, add=None, after=(), hold=()):
    has_add = add is not None
    adds = [add] if has_add else []
    scratch = [pltpu.VMEM((CAP, C), BF), pltpu.VMEM((PIX, CAP), BF)]
    if has_add:
        scratch += [pltpu.VMEM((PIX, C), BF), pltpu.SemaphoreType.DMA]
    return pl.pallas_call(
        functools.partial(sum_kernel, which, has_add),
        out_shape=[jax.ShapeDtypeStruct((PIX, C), BF), jax.ShapeDtypeStruct((8, 128), F32)],
        in_specs=[SM, VM, VM, VM] + [HB] * len(adds) + [VM] * len(after) + [HB] * len(hold),
        out_specs=[VM, VM],
        scratch_shapes=scratch,
        compiler_params=params(30),
        cost_estimate=cost(2**29, 2**19),
    )(flags, idx, table, ask, *adds, *after, *hold)


PUT = 1024


def scatter_kernel(blocks, halves, has_add, flags, idx_ref, *rest):
    n = len(blocks)
    asks = rest[:n]
    rest = rest[n:]
    grads = []
    for h in halves:
        grads.append(rest[:h])
        rest = rest[h:]
    if has_add:
        add_ref = rest[0]
    out_ref, done_ref, slot_ref = rest[-3:]

    def spread(row, rows, dtype):
        tall = jnp.broadcast_to(row, (16, KC)).astype(dtype)
        return jnp.broadcast_to(tall[None], (rows // 16, 16, KC)).reshape(rows, KC)

    @pl.when(pl.program_id(0) == 0)
    def _():
        base = lanes_iota((MT, KC), 0, I16)
        zero = jnp.zeros((MT, KC), BF)
        for i in range(n):
            group = (flags[GROUP + blocks[i]] * CAP).astype(F32)
            who = flags[WHOSE + blocks[i]]

            def mixed(m, carry):
                first = group + (m * MT).astype(F32)
                acc = jnp.zeros((MT, C), F32)
                for q in range(PIX // KC):
                    lanes = slice(q * KC, (q + 1) * KC)
                    w = None
                    for k in range(4):
                        slots = spread((asks[i][who, k : k + 1, lanes] - first).astype(I32), MT, I16)
                        term = jnp.where(slots == base, spread(asks[i][who, 4 + k : 5 + k, lanes], MT, BF), zero)
                        w = term if w is None else w + term
                    part = PIX // halves[i]
                    ref = grads[i][q * KC // part]
                    at = q * KC % part
                    acc = acc + jnp.dot(w, ref[at : at + KC, :], preferred_element_type=F32)
                slot_ref[pl.ds(pl.multiple_of(i * CAP + m * MT, MT), MT), :] = acc.astype(BF)
                return carry

            lax.fori_loop(0, CAP // MT, mixed, 0)

    base = lanes_iota((PUT, KC), 0, I16)
    one = jnp.ones((PUT, KC), BF)
    zero = jnp.zeros((PUT, KC), BF)
    first = pl.program_id(0) * PUT
    acc = add_ref[...] if has_add else jnp.zeros((PUT, C), F32)
    for i in range(n):
        for q in range(CAP // KC):
            want = spread(idx_ref[blocks[i] : blocks[i] + 1, q * KC : (q + 1) * KC] - first, PUT, I16)
            hot = jnp.where(want == base, one, zero)
            at = i * CAP + q * KC
            acc = acc + jnp.dot(hot, slot_ref[at : at + KC, :], preferred_element_type=F32)
    out_ref[...] = acc.astype(out_ref.dtype)
    done_ref[...] = jnp.zeros_like(done_ref)


def row_grads(flags, idx, blocks, asks, grads, add, dtype, after=(), hold=()):
    n = len(blocks)
    has_add = add is not None
    grads = [g if isinstance(g, tuple) else (g,) for g in grads]
    halves = [len(g) for g in grads]
    whole = [idx, *asks] + [x for g in grads for x in g]
    tile = pl.BlockSpec((PUT, C), lambda m: (m, 0))
    specs = [SM] + [pl.BlockSpec(x.shape, lambda m, n=x.ndim: (0,) * n) for x in whole] + ([tile] if has_add else [])
    specs = specs + [VM] * len(after) + [HB] * len(hold)
    return pl.pallas_call(
        functools.partial(scatter_kernel, blocks, halves, has_add),
        grid=(ROWS // PUT,),
        out_shape=[jax.ShapeDtypeStruct((ROWS, C), dtype), jax.ShapeDtypeStruct((8, 128), F32)],
        in_specs=specs,
        out_specs=[tile, pl.BlockSpec((8, 128), lambda m: (0, 0))],
        scratch_shapes=[pltpu.VMEM((n * CAP, C), BF)],
        compiler_params=params(40),
        cost_estimate=cost(n * 2**29, 2**19),
    )(flags, *whole, *([add] if has_add else []), *after, *hold)


MARK = 16
STRIPS = 2 * TS + MARK
TAPS = 9 * C
PADDED = 2560
HALF, QUARTER, PIECE = PADDED // 2, PADDED // 8, PADDED // 32


def spread_rows(lines):
    rows = lines.shape[0]
    return jnp.broadcast_to(lines[:, None, :], (rows, TS, C)).reshape(rows * TS, C)


def split_lines(flags, north, south, west, east, inner_ref, outer_ref):
    top = flags[TOP] == 1
    left = flags[LEFT] == 1
    inner_ref[0] = jnp.where(top, south, north).astype(BF)
    inner_ref[1] = jnp.where(left, east, west).astype(BF)
    outer_ref[0:TS, :] = jnp.where(top, north, south).astype(BF)
    outer_ref[TS : 2 * TS, :] = jnp.where(left, west, east).astype(BF)


def join_lines(flags, in_rows, in_cols, parts):
    row = lax.broadcasted_iota(I32, (TS, TS), 0)
    col = lax.broadcasted_iota(I32, (TS, TS), 1)
    turn = (row + col == TS - 1).astype(BF)
    outer = []
    for s in range(2):
        line = jnp.zeros((TS, C), BF)
        for part in parts:
            at = part.shape[0] - 2 * TS + s * TS
            line = line + part[at : at + TS, :]
        back = jnp.dot(turn, line, preferred_element_type=F32)
        outer.append(jnp.where(flags[FLIP + s] == 1, back, line.astype(F32)))
    top = flags[TOP] == 1
    left = flags[LEFT] == 1
    in_rows = in_rows.astype(F32)
    in_cols = in_cols.astype(F32)
    north = jnp.where(top, outer[0], in_rows)
    south = jnp.where(top, in_rows, outer[0])
    west = jnp.where(left, outer[1], in_cols)
    east = jnp.where(left, in_cols, outer[1])
    return north, south, west, east


def call(kernel, outs, mib, flags, *operands, scratch=(), after=()):
    n, m = len(operands), len(after)

    def body(flags, *refs):
        kernel(flags, *refs[:n], *refs[n + m :])

    return pl.pallas_call(
        body,
        out_shape=[jax.ShapeDtypeStruct(shape, dtype) for shape, dtype in outs],
        in_specs=[SM] + [VM] * (n + m),
        out_specs=[VM] * len(outs),
        scratch_shapes=list(scratch),
        compiler_params=params(mib),
        cost_estimate=cost(2**20, 2**20),
    )(flags, *operands, *after)


def tie_kernel(*refs):
    pass


def tied(values, after):
    n = len(values)
    return pl.pallas_call(
        tie_kernel,
        out_shape=[jax.ShapeDtypeStruct(x.shape, x.dtype) for x in values],
        in_specs=[HB] * n + [VM] * len(after),
        out_specs=[HB] * n,
        input_output_aliases={i: i for i in range(n)},
        compiler_params=params(1),
        cost_estimate=cost(2**10, 2**10),
    )(*values, *after)


def line_places(face):
    core = jnp.bitwise_and(face, 1)
    x = jnp.bitwise_and(lax.shift_right_logical(face, 1), 3)
    z = lax.shift_right_logical(face, 3)
    return core, jnp.where(core == 0, z, x), jnp.where(core == 0, x, z)


def pick_strips(flags, sets, outs):
    face = flags[FACE]
    step = jnp.where(jnp.bitwise_and(face, 1) == 0, 2, 8)
    zero = jnp.zeros((TS, C), F32)
    want = [[zero, zero] for _ in range(4)]
    for ref, at in sets:
        for core in range(2):
            base = at + core * STRIPS
            for s in range(2):
                strip = ref[base + s * TS : base + (s + 1) * TS, :].astype(F32)
                mark = ref[base + 2 * TS : base + STRIPS, :].astype(F32)[s * 8 : s * 8 + 1, :]
                mark = jnp.broadcast_to(mark, (TS, C))
                for k in range(4):
                    for slot in range(2):
                        place = (jnp.bitwise_xor(face, step * k) * 2 + slot).astype(F32)
                        want[k][slot] = jnp.where(mark == place, strip, want[k][slot])
    for k in range(4):
        ref, at = outs[k]
        for slot in range(2):
            ref[at + slot * TS : at + (slot + 1) * TS, :] = want[k][slot].astype(BF)


def route_kernel(flags, own_ref, a_ref, b_ref, c_ref, *outs):
    pick_strips(flags, [(r, 0) for r in (own_ref, a_ref, b_ref, c_ref)], [(r, 0) for r in outs])


def exchange(flags, inner, outer):
    rows = lax.ppermute(inner[0], "tile", [(i, i ^ 2) for i in range(4)])
    cols = lax.ppermute(inner[1], "tile", [(i, i ^ 1) for i in range(4)])
    both = jnp.concatenate([outer, other_core(outer)])
    sets = [along_first(both, k) for k in (1, 2, 3)]
    sets, rows, cols = lax.optimization_barrier((sets, rows, cols))
    ways = call(route_kernel, [((2 * TS, C), BF)] * 4, 24, flags, both, *sets)
    return [rows, cols, ways[0]] + [along_second(ways[k], k) for k in (1, 2, 3)]


def tap_kernel(flags, p_ref, gp_ref, outer_ref, own_ref, send_ref, all_ref):
    turned = gp_ref[...].T
    for a in range(3):
        for b in range(3):
            at = (a * 3 + b) * C
            part = jnp.dot(turned, p_ref[b, a * TS : a * TS + PIX, :], preferred_element_type=F32)
            all_ref[at : at + C, :] = part.T
    bias = jnp.sum(gp_ref[...].astype(F32), axis=0, keepdims=True)
    row = lax.broadcasted_iota(I32, (PADDED - TAPS, C), 0)
    all_ref[TAPS:PADDED, :] = jnp.where(row == 0, bias, 0.0)
    core = jnp.bitwise_and(flags[FACE], 1)
    own_ref[...] = all_ref[pl.ds(pl.multiple_of(core * HALF, 64), HALF), :]
    send_ref[0:HALF, :] = all_ref[pl.ds(pl.multiple_of((1 - core) * HALF, 64), HALF), :].astype(BF)
    send_ref[HALF : HALF + STRIPS, :] = outer_ref[...]


def half_kernel(flags, own_ref, got_ref, outer_ref, piece_ref, *rest):
    sends = rest[:3]
    strips_ref, all_ref = rest[3:]
    all_ref[...] = own_ref[...] + got_ref[0:HALF, :].astype(F32)
    strips_ref[0:STRIPS, :] = outer_ref[...]
    strips_ref[STRIPS : 2 * STRIPS, :] = got_ref[HALF : HALF + STRIPS, :]
    _, first, _ = line_places(flags[FACE])
    for k in range(4):
        at = pl.multiple_of(jnp.bitwise_xor(first, k) * QUARTER, 64)
        part = all_ref[pl.ds(at, QUARTER), :]
        if k == 0:
            piece_ref[...] = part
        else:
            sends[k - 1][0:QUARTER, :] = part.astype(BF)
            sends[k - 1][QUARTER : QUARTER + 2 * STRIPS, :] = strips_ref[...]


def quarter_kernel(flags, piece_ref, strips_ref, a_ref, b_ref, c_ref, own_ref, out_ref, *rest):
    sends = rest[:3]
    all_ref = rest[3]
    got = [r[0:QUARTER, :].astype(F32) for r in (a_ref, b_ref, c_ref)]
    all_ref[...] = (piece_ref[...] + got[0]) + (got[1] + got[2])
    pick_strips(
        flags,
        [(strips_ref, 0)] + [(r, QUARTER) for r in (a_ref, b_ref, c_ref)],
        [(out_ref, 0)] + [(r, 2 * PIECE) for r in sends],
    )
    _, _, second = line_places(flags[FACE])
    for k in range(4):
        at = pl.multiple_of(jnp.bitwise_xor(second, k) * PIECE, 16)
        part = all_ref[pl.ds(at, PIECE), :]
        if k == 0:
            own_ref[...] = part
        else:
            high = part.astype(BF)
            sends[k - 1][0:PIECE, :] = high
            sends[k - 1][PIECE : 2 * PIECE, :] = (part - high.astype(F32)).astype(BF)


def two_part(ref):
    return ref[0:PIECE, :].astype(F32) + ref[PIECE : 2 * PIECE, :].astype(F32)


def piece_kernel(flags, own_ref, a_ref, b_ref, c_ref, in_ref, cols_ref, rows_ref, both_ref):
    part = (own_ref[...] + two_part(a_ref)) + (two_part(b_ref) + two_part(c_ref))
    high = part.astype(BF)
    both_ref[0:PIECE, :] = high
    both_ref[PIECE : 2 * PIECE, :] = (part - high.astype(F32)).astype(BF)
    for ref, line in ((cols_ref, in_ref[1]), (rows_ref, in_ref[0])):
        ref[0 : 2 * PIECE, :] = both_ref[...]
        ref[2 * PIECE : 2 * PIECE + TS, :] = line


def exchange_and_sum(flags, inner, outer, windows, grad_pre):
    own, send = call(
        tap_kernel, [((HALF, C), F32), ((HALF + STRIPS, C), BF)], 30, flags, windows, grad_pre, outer,
        scratch=[pltpu.VMEM((PADDED, C), F32)],
    )
    piece, a, b, c, strips = call(
        half_kernel, [((QUARTER, C), F32)] + [((QUARTER + 2 * STRIPS, C), BF)] * 3 + [((2 * STRIPS, C), BF)],
        24, flags, own, other_core(send), outer, scratch=[pltpu.VMEM((HALF, C), F32)],
    )
    own, out, d, e, f = call(
        quarter_kernel, [((PIECE, C), F32), ((2 * TS, C), BF)] + [((2 * PIECE + 2 * TS, C), BF)] * 3,
        24, flags, piece, strips, along_first(a, 1), along_first(b, 2), along_first(c, 3),
        scratch=[pltpu.VMEM((QUARTER, C), F32)],
    )
    d, e, f = along_second(d, 1), along_second(e, 2), along_second(f, 3)
    cols, rows, both = call(
        piece_kernel, [((2 * PIECE + TS, C), BF)] * 2 + [((2 * PIECE, C), BF)], 24, flags, own, d, e, f, inner
    )
    return (both, along_tile(cols, 1), along_tile(rows, 2), along_tile(both, 3)), (out, d, e, f)


LINES = [jax.ShapeDtypeStruct((2, TS, C), BF), jax.ShapeDtypeStruct((STRIPS, C), BF)]


def field_kernel(flags, mark_ref, a_ref, b_ref, c_ref, d_ref, field_ref, inner_ref, outer_ref):
    total = a_ref[...].astype(F32) + b_ref[...].astype(F32) + c_ref[...].astype(F32) + d_ref[...].astype(F32)
    outer_ref[2 * TS : STRIPS, :] = mark_ref[...]
    field_ref[...] = total.astype(BF)
    grid = total.reshape(TS, TS, C)
    split_lines(flags, total[0:TS], total[PIX - TS : PIX], grid[:, 0, :], grid[:, TS - 1, :], inner_ref, outer_ref)


def make_field(flags, marks, parts):
    return pl.pallas_call(
        field_kernel,
        out_shape=[jax.ShapeDtypeStruct((PIX, C), BF)] + LINES,
        in_specs=[SM] + [VM] * 5,
        out_specs=[VM] * 3,
        compiler_params=params(24),
        cost_estimate=cost(2**20, 3 * 2**20),
    )(flags, marks, *parts)


def conv_kernel(flags, field_ref, mark_ref, rows_ref, cols_ref, s0_ref, s1_ref, s2_ref, s3_ref, w_ref, bias_ref, cot_ref,
                act_ref, gp_ref, p_ref, mid_ref, inner_ref, outer_ref, q_ref, gf_ref):
    n = 34 * TS
    north, south, west, east = join_lines(flags, rows_ref[...], cols_ref[...], (s0_ref, s1_ref, s2_ref, s3_ref))
    outer_ref[2 * TS : STRIPS, :] = mark_ref[...]
    zero = jnp.zeros((1, C), F32)
    p_ref[1, 0:TS, :] = north.astype(BF)
    p_ref[1, TS : TS + PIX, :] = field_ref[...]
    p_ref[1, TS + PIX : n, :] = south.astype(BF)
    x = p_ref[1].astype(F32)
    col = lax.broadcasted_iota(I32, (n, C), 0) % TS
    west = jnp.concatenate([zero, west, zero])
    east = jnp.concatenate([zero, east, zero])
    p_ref[0] = jnp.where(col == 0, spread_rows(west), pltpu.roll(x, 1, 0)).astype(BF)
    p_ref[2] = jnp.where(col == TS - 1, spread_rows(east), pltpu.roll(x, n - 1, 0)).astype(BF)
    step = 256
    q_ref[1, 0 : 2 * TS, :] = jnp.zeros((2 * TS, C), BF)
    q_ref[1, 2 * TS + PIX : 4 * TS + PIX, :] = jnp.zeros((2 * TS, C), BF)
    for m in range(PIX // step):
        rows = slice(m * step, (m + 1) * step)
        pre = jnp.broadcast_to(bias_ref[...], (step, C))
        for a in range(3):
            for b in range(3):
                pre = pre + jnp.dot(
                    p_ref[b, a * TS + m * step : a * TS + (m + 1) * step, :], w_ref[a, b], preferred_element_type=F32
                )
        cdf = 0.5 * (1.0 + lax.erf(pre * root_half))
        act_ref[rows, :] = (pre * cdf).astype(BF)
        slope = cdf + pre * inv_root_two_pi * jnp.exp(-0.5 * pre * pre)
        g = (cot_ref[rows, :].astype(F32) * slope).astype(BF)
        gp_ref[rows, :] = g
        q_ref[1, 2 * TS + m * step : 2 * TS + (m + 1) * step, :] = g
        gf_ref[rows, :] = g.astype(F32)
    nq = 36 * TS
    y = q_ref[1].astype(F32)
    colq = lax.broadcasted_iota(I32, (nq, C), 0) % TS
    q_ref[0] = jnp.where(colq == TS - 1, 0.0, pltpu.roll(y, nq - 1, 0)).astype(BF)
    q_ref[2] = jnp.where(colq == 0, 0.0, pltpu.roll(y, 1, 0)).astype(BF)

    def back(r0, rows):
        acc = jnp.zeros((rows, C), F32)
        for a in range(3):
            for b in range(3):
                first = (2 - a) * TS + r0
                acc = acc + lax.dot_general(q_ref[b, first : first + rows, :], w_ref[a, b], NT, preferred_element_type=F32)
        return acc

    rid = lax.broadcasted_iota(I32, (TS, C), 0)
    sides = []
    for c, b in ((0, 0), (TS - 1, 2)):
        e = gf_ref[...].reshape(TS, TS, C)[:, c, :]
        up = jnp.where(rid == TS - 1, 0.0, pltpu.roll(e, TS - 1, 0))
        down = jnp.where(rid == 0, 0.0, pltpu.roll(e, 1, 0))
        acc = jnp.zeros((TS, C), F32)
        for a, v in ((0, up), (1, e), (2, down)):
            acc = acc + lax.dot_general(v.astype(BF), w_ref[a, b], NT, preferred_element_type=F32)
        sides.append(acc)
    split_lines(flags, back(0, TS), back(33 * TS, TS), sides[0], sides[1], inner_ref, outer_ref)
    for m in range(PIX // step):
        mid_ref[m * step : (m + 1) * step, :] = back(TS + m * step, step)


def conv(flags, field, marks, edges, w, bias, cot):
    return pl.pallas_call(
        conv_kernel,
        out_shape=[
            jax.ShapeDtypeStruct((PIX, C), BF),
            jax.ShapeDtypeStruct((PIX, C), BF),
            jax.ShapeDtypeStruct((3, 34 * TS, C), BF),
            jax.ShapeDtypeStruct((PIX, C), F32),
        ] + LINES,
        in_specs=[SM] + [VM] * 11,
        out_specs=[VM] * 6,
        scratch_shapes=[pltpu.VMEM((3, 36 * TS, C), BF), pltpu.VMEM((PIX, C), F32)],
        compiler_params=params(40),
        cost_estimate=cost(2**29, 2**19),
    )(flags, field, marks, *edges, w, bias, cot)


def total_kernel(flags, mid_ref, y1_ref, y2_ref, s0_ref, s1_ref, s2_ref, s3_ref, out_ref):
    cols = y1_ref[2 * PIECE : 2 * PIECE + TS, :]
    rows = y2_ref[2 * PIECE : 2 * PIECE + TS, :]
    north, south, west, east = join_lines(flags, rows, cols, (s0_ref, s1_ref, s2_ref, s3_ref))
    col = lax.broadcasted_iota(I32, (PIX, C), 0) % TS
    x = mid_ref[...]
    x = x + jnp.where(col == 0, spread_rows(west), 0.0) + jnp.where(col == TS - 1, spread_rows(east), 0.0)
    out_ref[...] = x.astype(BF)
    out_ref[0:TS, :] = (x[0:TS] + north).astype(BF)
    out_ref[PIX - TS : PIX, :] = (x[PIX - TS : PIX] + south).astype(BF)


def piece_sum_kernel(flags, y0_ref, y1_ref, y2_ref, y3_ref, taps_ref):
    taps_ref[...] = ((two_part(y0_ref) + two_part(y1_ref)) + (two_part(y2_ref) + two_part(y3_ref))).astype(BF)


def join_kernel(flags, *refs):
    out_ref = refs[-1]
    size = refs[0].shape[0]
    for k in range(4):
        out_ref[k * size : (k + 1) * size, :] = refs[k][...]


def joined(flags, parts, after):
    size = parts[0].shape[0]
    return call(join_kernel, [((4 * size, C), BF)], 24, flags, *parts, after=after)[0]


def place_kernel(flags, own_ref, twin_ref, taps_ref, bias_ref, all_ref):
    face = flags[FACE]
    for c, ref in ((0, own_ref), (1, twin_ref)):
        for k in range(16):
            core, first, second = line_places(jnp.bitwise_xor(face, c))
            at = core * HALF + jnp.bitwise_xor(first, k >> 2) * QUARTER + jnp.bitwise_xor(second, k & 3) * PIECE
            all_ref[pl.ds(pl.multiple_of(at, 16), PIECE), :] = ref[k * PIECE : (k + 1) * PIECE, :].astype(F32)
    taps_ref[...] = all_ref[0:TAPS, :]
    bias_ref[...] = all_ref[TAPS : TAPS + 8, :][0:1, :]


def place_taps(flags, own, twin):
    taps, bias = call(
        place_kernel, [((TAPS, C), F32), ((1, C), F32)], 24, flags, own, twin, scratch=[pltpu.VMEM((PADDED, C), F32)]
    )
    return taps.reshape(3, 3, C, C), bias[0]


def shards(latlon, send_rows, send_count, interp_slot, interp_weight, outer_partner, outer_side, outer_flip,
           conv_weight, conv_bias, cotangent):
    faces = lax.axis_size("face")
    face = lax.axis_index("face")
    j = lax.axis_index("tile")
    steps = jnp.arange(4, dtype=I32)
    owner = j ^ steps
    group = jnp.concatenate([4 + j - owner, (j - owner) % 8])

    mine = jnp.concatenate([interp_slot.T.astype(F32), interp_weight.T])
    trio = jnp.stack([mine, from_face(mine, 1, faces), from_face(mine, -1, faces)])
    ask = [trio] + [along_tile(trio, k) for k in (1, 2, 3)]
    live = jnp.arange(CAP, dtype=I32)[None, :] < send_count[0][:, None]
    idx = jnp.where(live, send_rows[0], -1)[group]
    idx_cols = idx.T

    goal = outer_partner[0, 0] * 2 + outer_side[0, 0]
    marks = jnp.broadcast_to(jnp.repeat(goal, MARK // 2)[:, None], (MARK, C)).astype(BF)
    corner = jnp.stack([(j // 2 == 0), (j % 2 == 0)])
    whose = jnp.where(owner <= j, 1, 2)
    flags = jnp.concatenate(
        [jnp.stack([face, j]), outer_flip[0, 0], corner.astype(I32), group, jnp.zeros((4,), I32), whose]
    ).astype(I32)

    far = [None] * 4

    ask = ask + ask
    part, done = partial_sum(flags, 6, idx_cols, latlon, ask[6], after=[ask[1], ask[3]])
    far[2] = to_far(part, 2, faces)
    part, done = partial_sum(flags, 5, idx_cols, latlon, ask[5], after=[done])
    far[1] = to_far(part, 1, faces)
    part, done = partial_sum(flags, 7, idx_cols, latlon, ask[7], after=[done])
    far[3] = to_far(part, 3, faces)
    part, done = partial_sum(flags, 2, idx_cols, latlon, ask[2], far[2], [done])
    across = along_tile(part, 2)
    part, done = partial_sum(flags, 4, idx_cols, latlon, ask[4], after=[done])
    far[0] = to_far(part, 0, faces)
    part, done = partial_sum(flags, 1, idx_cols, latlon, ask[1], far[1], [done])
    up = along_tile(part, 1)
    part, done = partial_sum(flags, 3, idx_cols, latlon, ask[3], far[3], [done])
    down = along_tile(part, 3)
    part, done = partial_sum(flags, 0, idx_cols, latlon, ask[0], far[0], [done], [across])
    moved = [across, up, down]
    field, inner, outer = make_field(flags, marks, [part] + moved)
    edges = exchange(flags, inner, outer)
    activated, grad_pre, windows, mid, inner, outer = conv(
        flags, field, marks, edges, conv_weight, conv_bias[None, :], cotangent
    )
    lines, strips = exchange_and_sum(flags, inner, outer, windows, grad_pre)
    whole, = call(
        total_kernel, [((PIX, C), BF)], 24, flags, mid, lines[1], lines[2], *strips, after=[lines[3]]
    )
    up = along_tile(whole, 1)
    down = along_tile(whole, 3)
    far0 = from_far(whole, 0, faces)
    rows, done = row_grads(flags, idx, (0,), (ask[0],), (whole,), None, F32)
    rows, done = row_grads(flags, idx, (4,), (ask[4],), (far0,), rows, F32)
    up, down, whole = tied([up, down, whole], [done])
    across = along_tile(whole, 2)
    far1 = from_far(up, 1, faces)
    far3 = from_far(down, 3, faces)
    rows, done = row_grads(flags, idx, (1, 3), (ask[1], ask[3]), (up, down), rows, F32)
    across, = tied([across], [done])
    far2 = from_far(across, 2, faces)
    taps, = call(piece_sum_kernel, [((PIECE, C), BF)], 24, flags, *lines, after=[done])
    moved = [along_second(taps, k) for k in (1, 2, 3)]
    rows, done = row_grads(flags, idx, (5, 7), (ask[5], ask[7]), (far1, far3), rows, F32)
    line = joined(flags, [taps] + moved, [done])
    moved = [along_first(line, k) for k in (1, 2, 3)]
    rows, done = row_grads(flags, idx, (2,), (ask[2],), (across,), rows, F32, hold=[far2])
    taps = joined(flags, [line] + moved, [done])
    twin = other_core(taps)
    grad_latlon, done = row_grads(flags, idx, (6,), (ask[6],), (far2,), rows, BF)
    grad_weight, grad_bias = place_taps(flags, taps, twin)
    return activated, grad_latlon, grad_weight, grad_bias


def solution(mesh):
    both = ("face", "tile")
    placed = (
        P(both, None), P(both, None, None), P(both, None), P(both, None), P(both, None),
        P("face", "tile", None), P("face", "tile", None), P("face", "tile", None), P(), P(), P(both, None),
    )
    return jax.shard_map(
        shards, mesh=mesh, in_specs=placed, out_specs=(P(both, None), P(both, None), P(), P()), check_vma=False
    )
```

```python
import functools
import jax
import jax.numpy as jnp
from jax import lax
from jax.experimental import pallas as pl
from jax.experimental.pallas import tpu as pltpu
from jax.sharding import PartitionSpec as P

BF = jnp.bfloat16
F32 = jnp.float32
I16 = jnp.int16
I32 = jnp.int32
AXES = ("face", "tile")
TS = 32
PIX = 1024
CAP = 1024
ROWS = 4096
C = 256
MT = 512
KC = 256

FACE, TILE, FLIP, TOP, LEFT, GROUP, WHOSE = 0, 1, 2, 4, 5, 6, 14

root_half = 0.7071067811865476
inv_root_two_pi = 0.3989422804014327
VM = pl.BlockSpec(memory_space=pltpu.VMEM)
SM = pl.BlockSpec(memory_space=pltpu.SMEM)
HB = pl.BlockSpec(memory_space=pl.ANY)
NT = (((1,), (1,)), ((), ()))


def params(mib):
    return pltpu.CompilerParams(vmem_limit_bytes=mib * 2**20)


def cost(flops, size):
    return pl.CostEstimate(flops=flops, bytes_accessed=size, transcendentals=0)


def far_face(j, k):
    return 1 if j ^ k <= j else -1


def to_far(value, k, faces):
    pairs = []
    for face in range(faces):
        for j in range(4):
            pairs.append((face * 4 + j, (face + far_face(j, k)) % faces * 4 + j))
    return lax.ppermute(value, AXES, pairs)


def from_far(value, k, faces):
    pairs = []
    for face in range(faces):
        for j in range(4):
            pairs.append(((face + far_face(j, k)) % faces * 4 + j, face * 4 + j))
    return lax.ppermute(value, AXES, pairs)


def from_face(value, step, faces):
    return lax.ppermute(value, "face", [((i + step) % faces, i) for i in range(faces)])


def along_tile(value, k):
    return lax.ppermute(value, "tile", [(i, i ^ k) for i in range(4)])


def first_step(i):
    return 2 if i & 1 else 8


def second_step(i):
    return 8 if i & 1 else 2


def along_first(value, k):
    return lax.ppermute(value, "face", [(i, i ^ (k * first_step(i))) for i in range(32)])


def along_second(value, k):
    return lax.ppermute(value, "face", [(i, i ^ (k * second_step(i))) for i in range(32)])


def other_core(value):
    return lax.ppermute(value, "face", [(i, i ^ 1) for i in range(32)])


def gate(value, after):
    return lax.optimization_barrier((value, after))


def lanes_iota(shape, dim, dtype):
    return lax.broadcasted_iota(I32, shape, dim).astype(dtype)


def pick_rows(want, table_ref):
    base = lanes_iota((MT, KC), 1, I16)
    one = jnp.ones((MT, KC), BF)
    zero = jnp.zeros((MT, KC), BF)
    want = jnp.concatenate([jnp.broadcast_to(want, (MT, 128)).astype(I16)] * (KC // 128), axis=1)
    acc = jnp.zeros((MT, C), F32)
    for k in range(ROWS // KC):
        hot = jnp.where(want == base + jnp.asarray(k * KC, I16), one, zero)
        acc = acc + jnp.dot(hot, table_ref[k * KC : (k + 1) * KC, :], preferred_element_type=F32)
    return acc.astype(BF)


SUB = 64


def weigh(first, ask, w_ref):
    base = lanes_iota((SUB, 128), 1, I16)
    zero = jnp.zeros((SUB, 128), BF)
    row = lax.broadcasted_iota(I32, (8, PIX), 0)
    ask = jnp.where(row < 4, ask - first, ask).T
    for p in range(0, PIX, SUB):
        slots = [jnp.broadcast_to(ask[p : p + SUB, k : k + 1], (SUB, 128)).astype(I32).astype(I16) for k in range(4)]
        scale = [jnp.broadcast_to(ask[p : p + SUB, 4 + k : 5 + k], (SUB, 128)).astype(BF) for k in range(4)]
        for q in range(0, CAP, 128):
            here = base + jnp.asarray(q, I16)
            w = jnp.where(slots[0] == here, scale[0], zero)
            for k in range(1, 4):
                w = w + jnp.where(slots[k] == here, scale[k], zero)
            w_ref[p : p + SUB, q : q + 128] = w


def sum_kernel(which, has_add, given, flags, *refs):
    out_ref, done_ref = refs[-4:-2] if not given else refs[-3:-1]
    w_ref = refs[-1]
    if given:
        got_ref, ask_ref = refs[:2]
    else:
        idx_ref, table_ref, ask_ref = refs[:3]
        got_ref = refs[-2]
    done_ref[...] = jnp.zeros_like(done_ref)
    weigh((flags[GROUP + which] * CAP).astype(F32), ask_ref[flags[WHOSE + which]], w_ref)
    if not given:
        for m in range(0, CAP, MT):
            got_ref[m : m + MT, :] = pick_rows(idx_ref[m : m + MT, which : which + 1], table_ref)
    for m in range(0, PIX, MT):
        acc = refs[3][m : m + MT, :].astype(F32) if has_add else jnp.zeros((MT, C), F32)
        for q in range(0, CAP, KC):
            acc = acc + jnp.dot(w_ref[m : m + MT, q : q + KC], got_ref[q : q + KC, :], preferred_element_type=F32)
        out_ref[m : m + MT, :] = acc.astype(BF)


def sum_call(flags, which, has_add, given, operands, after, hold):
    scratch = [] if given else [pltpu.VMEM((CAP, C), BF)]
    return pl.pallas_call(
        functools.partial(sum_kernel, which, has_add, given),
        out_shape=[jax.ShapeDtypeStruct((PIX, C), BF), jax.ShapeDtypeStruct((8, 128), F32)],
        in_specs=[SM] + [VM] * (len(operands) + len(after)) + [HB] * len(hold),
        out_specs=[VM, VM],
        scratch_shapes=scratch + [pltpu.VMEM((PIX, CAP), BF)],
        compiler_params=params(30),
        cost_estimate=cost(2**29, 2**19),
    )(flags, *operands, *after, *hold)


def partial_sum(flags, which, idx, table, ask, add=None, after=(), hold=()):
    adds = [] if add is None else [add]
    return sum_call(flags, which, bool(adds), False, [idx, table, ask, *adds], after, hold)


def gather_kernel(picks, idx_ref, table_ref, *outs):
    for b, out_ref in zip(picks, outs):
        for m in range(0, CAP, MT):
            out_ref[m : m + MT, :] = pick_rows(idx_ref[m : m + MT, b : b + 1], table_ref)


def gather_rows(picks, idx, table):
    n = len(picks)
    return pl.pallas_call(
        functools.partial(gather_kernel, picks),
        out_shape=[jax.ShapeDtypeStruct((CAP, C), BF)] * n,
        in_specs=[VM] * 2,
        out_specs=[VM] * n,
        compiler_params=params(24),
        cost_estimate=cost(n * 2**29, 2**19),
    )(idx, table)


def mix(flags, which, ask, got, after=()):
    return sum_call(flags, which, False, True, [got, ask], after, ())


PUT = 1024


def scatter_kernel(blocks, halves, has_add, flags, idx_ref, *rest):
    n = len(blocks)
    asks = rest[:n]
    rest = rest[n:]
    grads = []
    for h in halves:
        grads.append(rest[:h])
        rest = rest[h:]
    if has_add:
        add_ref = rest[0]
    out_ref, done_ref, slot_ref = rest[-3:]

    def spread(row, rows, dtype):
        tall = jnp.broadcast_to(row, (16, KC)).astype(dtype)
        return jnp.broadcast_to(tall[None], (rows // 16, 16, KC)).reshape(rows, KC)

    @pl.when(pl.program_id(0) == 0)
    def _():
        base = lanes_iota((MT, KC), 0, I16)
        zero = jnp.zeros((MT, KC), BF)
        for i in range(n):
            group = (flags[GROUP + blocks[i]] * CAP).astype(F32)
            who = flags[WHOSE + blocks[i]]

            def mixed(m, carry):
                first = group + (m * MT).astype(F32)
                acc = jnp.zeros((MT, C), F32)
                for q in range(PIX // KC):
                    lanes = slice(q * KC, (q + 1) * KC)
                    w = None
                    for k in range(4):
                        slots = spread((asks[i][who, k : k + 1, lanes] - first).astype(I32), MT, I16)
                        term = jnp.where(slots == base, spread(asks[i][who, 4 + k : 5 + k, lanes], MT, BF), zero)
                        w = term if w is None else w + term
                    part = PIX // halves[i]
                    ref = grads[i][q * KC // part]
                    at = q * KC % part
                    acc = acc + jnp.dot(w, ref[at : at + KC, :], preferred_element_type=F32)
                slot_ref[pl.ds(pl.multiple_of(i * CAP + m * MT, MT), MT), :] = acc.astype(BF)
                return carry

            lax.fori_loop(0, CAP // MT, mixed, 0)

    base = lanes_iota((PUT, KC), 0, I16)
    one = jnp.ones((PUT, KC), BF)
    zero = jnp.zeros((PUT, KC), BF)
    first = pl.program_id(0) * PUT
    acc = add_ref[...] if has_add else jnp.zeros((PUT, C), F32)
    for i in range(n):
        for q in range(CAP // KC):
            want = spread(idx_ref[blocks[i] : blocks[i] + 1, q * KC : (q + 1) * KC] - first, PUT, I16)
            hot = jnp.where(want == base, one, zero)
            at = i * CAP + q * KC
            acc = acc + jnp.dot(hot, slot_ref[at : at + KC, :], preferred_element_type=F32)
    out_ref[...] = acc.astype(out_ref.dtype)
    done_ref[...] = jnp.zeros_like(done_ref)


def row_grads(flags, idx, blocks, asks, grads, add, dtype, after=(), hold=()):
    n = len(blocks)
    has_add = add is not None
    grads = [g if isinstance(g, tuple) else (g,) for g in grads]
    halves = [len(g) for g in grads]
    whole = [idx, *asks] + [x for g in grads for x in g]
    tile = pl.BlockSpec((PUT, C), lambda m: (m, 0))
    specs = [SM] + [pl.BlockSpec(x.shape, lambda m, n=x.ndim: (0,) * n) for x in whole] + ([tile] if has_add else [])
    specs = specs + [VM] * len(after) + [HB] * len(hold)
    return pl.pallas_call(
        functools.partial(scatter_kernel, blocks, halves, has_add),
        grid=(ROWS // PUT,),
        out_shape=[jax.ShapeDtypeStruct((ROWS, C), dtype), jax.ShapeDtypeStruct((8, 128), F32)],
        in_specs=specs,
        out_specs=[tile, pl.BlockSpec((8, 128), lambda m: (0, 0))],
        scratch_shapes=[pltpu.VMEM((n * CAP, C), BF)],
        compiler_params=params(40),
        cost_estimate=cost(n * 2**29, 2**19),
    )(flags, *whole, *([add] if has_add else []), *after, *hold)


MARK = 16
STRIPS = 2 * TS + MARK
TAPS = 9 * C
PADDED = 2560
HALF, QUARTER, PIECE = PADDED // 2, PADDED // 8, PADDED // 32


def spread_rows(lines):
    rows = lines.shape[0]
    return jnp.broadcast_to(lines[:, None, :], (rows, TS, C)).reshape(rows * TS, C)


def split_lines(flags, north, south, west, east, inner_ref, outer_ref):
    top = flags[TOP] == 1
    left = flags[LEFT] == 1
    inner_ref[0] = jnp.where(top, south, north).astype(BF)
    inner_ref[1] = jnp.where(left, east, west).astype(BF)
    outer_ref[0:TS, :] = jnp.where(top, north, south).astype(BF)
    outer_ref[TS : 2 * TS, :] = jnp.where(left, west, east).astype(BF)


def join_lines(flags, in_rows, in_cols, parts):
    row = lax.broadcasted_iota(I32, (TS, TS), 0)
    col = lax.broadcasted_iota(I32, (TS, TS), 1)
    turn = (row + col == TS - 1).astype(BF)
    outer = []
    for s in range(2):
        line = jnp.zeros((TS, C), BF)
        for part in parts:
            at = part.shape[0] - 2 * TS + s * TS
            line = line + part[at : at + TS, :]
        back = jnp.dot(turn, line, preferred_element_type=F32)
        outer.append(jnp.where(flags[FLIP + s] == 1, back, line.astype(F32)))
    top = flags[TOP] == 1
    left = flags[LEFT] == 1
    in_rows = in_rows.astype(F32)
    in_cols = in_cols.astype(F32)
    north = jnp.where(top, outer[0], in_rows)
    south = jnp.where(top, in_rows, outer[0])
    west = jnp.where(left, outer[1], in_cols)
    east = jnp.where(left, in_cols, outer[1])
    return north, south, west, east


def call(kernel, outs, mib, flags, *operands, scratch=(), after=(), hold=()):
    n, m = len(operands), len(after) + len(hold)

    def body(flags, *refs):
        kernel(flags, *refs[:n], *refs[n + m :])

    return pl.pallas_call(
        body,
        out_shape=[jax.ShapeDtypeStruct(shape, dtype) for shape, dtype in outs],
        in_specs=[SM] + [VM] * (n + len(after)) + [HB] * len(hold),
        out_specs=[VM] * len(outs),
        scratch_shapes=list(scratch),
        compiler_params=params(mib),
        cost_estimate=cost(2**20, 2**20),
    )(flags, *operands, *after, *hold)


def tie_kernel(*refs):
    pass


def tied(values, after):
    n = len(values)
    return pl.pallas_call(
        tie_kernel,
        out_shape=[jax.ShapeDtypeStruct(x.shape, x.dtype) for x in values],
        in_specs=[HB] * n + [VM] * len(after),
        out_specs=[HB] * n,
        input_output_aliases={i: i for i in range(n)},
        compiler_params=params(1),
        cost_estimate=cost(2**10, 2**10),
    )(*values, *after)


def line_places(face):
    core = jnp.bitwise_and(face, 1)
    x = jnp.bitwise_and(lax.shift_right_logical(face, 1), 3)
    z = lax.shift_right_logical(face, 3)
    return core, jnp.where(core == 0, z, x), jnp.where(core == 0, x, z)


def pick_strips(flags, sets, outs):
    face = flags[FACE]
    step = jnp.where(jnp.bitwise_and(face, 1) == 0, 2, 8)
    zero = jnp.zeros((TS, C), F32)
    want = [[zero, zero] for _ in range(4)]
    for ref, at in sets:
        for core in range(2):
            base = at + core * STRIPS
            for s in range(2):
                strip = ref[base + s * TS : base + (s + 1) * TS, :].astype(F32)
                mark = ref[base + 2 * TS : base + STRIPS, :].astype(F32)[s * 8 : s * 8 + 1, :]
                mark = jnp.broadcast_to(mark, (TS, C))
                for k in range(4):
                    for slot in range(2):
                        place = (jnp.bitwise_xor(face, step * k) * 2 + slot).astype(F32)
                        want[k][slot] = jnp.where(mark == place, strip, want[k][slot])
    for k in range(4):
        ref, at = outs[k]
        for slot in range(2):
            ref[at + slot * TS : at + (slot + 1) * TS, :] = want[k][slot].astype(BF)


def route_kernel(flags, own_ref, a_ref, b_ref, c_ref, *outs):
    pick_strips(flags, [(r, 0) for r in (own_ref, a_ref, b_ref, c_ref)], [(r, 0) for r in outs])


def exchange(flags, inner, outer):
    rows = lax.ppermute(inner[0], "tile", [(i, i ^ 2) for i in range(4)])
    cols = lax.ppermute(inner[1], "tile", [(i, i ^ 1) for i in range(4)])
    both = jnp.concatenate([outer, other_core(outer)])
    sets = [along_first(both, k) for k in (1, 2, 3)]
    sets, rows, cols = lax.optimization_barrier((sets, rows, cols))
    ways = call(route_kernel, [((2 * TS, C), BF)] * 4, 24, flags, both, *sets)
    return [rows, cols, ways[0]] + [along_second(ways[k], k) for k in (1, 2, 3)]


def tap_kernel(flags, p_ref, gp_ref, outer_ref, own_ref, send_ref, all_ref):
    turned = gp_ref[...].T
    for a in range(3):
        for b in range(3):
            at = (a * 3 + b) * C
            part = jnp.dot(turned, p_ref[b, a * TS : a * TS + PIX, :], preferred_element_type=F32)
            all_ref[at : at + C, :] = part.T
    bias = jnp.sum(gp_ref[...].astype(F32), axis=0, keepdims=True)
    row = lax.broadcasted_iota(I32, (PADDED - TAPS, C), 0)
    all_ref[TAPS:PADDED, :] = jnp.where(row == 0, bias, 0.0)
    core = jnp.bitwise_and(flags[FACE], 1)
    own_ref[...] = all_ref[pl.ds(pl.multiple_of(core * HALF, 64), HALF), :]
    send_ref[0:HALF, :] = all_ref[pl.ds(pl.multiple_of((1 - core) * HALF, 64), HALF), :].astype(BF)
    send_ref[HALF : HALF + STRIPS, :] = outer_ref[...]


def half_kernel(flags, own_ref, got_ref, outer_ref, piece_ref, *rest):
    sends = rest[:3]
    strips_ref, all_ref = rest[3:]
    all_ref[...] = own_ref[...] + got_ref[0:HALF, :].astype(F32)
    strips_ref[0:STRIPS, :] = outer_ref[...]
    strips_ref[STRIPS : 2 * STRIPS, :] = got_ref[HALF : HALF + STRIPS, :]
    _, first, _ = line_places(flags[FACE])
    for k in range(4):
        at = pl.multiple_of(jnp.bitwise_xor(first, k) * QUARTER, 64)
        part = all_ref[pl.ds(at, QUARTER), :]
        if k == 0:
            piece_ref[...] = part
        else:
            sends[k - 1][0:QUARTER, :] = part.astype(BF)
            sends[k - 1][QUARTER : QUARTER + 2 * STRIPS, :] = strips_ref[...]


def quarter_kernel(flags, piece_ref, strips_ref, a_ref, b_ref, c_ref, own_ref, out_ref, *rest):
    sends = rest[:3]
    all_ref = rest[3]
    got = [r[0:QUARTER, :].astype(F32) for r in (a_ref, b_ref, c_ref)]
    all_ref[...] = (piece_ref[...] + got[0]) + (got[1] + got[2])
    pick_strips(
        flags,
        [(strips_ref, 0)] + [(r, QUARTER) for r in (a_ref, b_ref, c_ref)],
        [(out_ref, 0)] + [(r, 2 * PIECE) for r in sends],
    )
    _, _, second = line_places(flags[FACE])
    for k in range(4):
        at = pl.multiple_of(jnp.bitwise_xor(second, k) * PIECE, 16)
        part = all_ref[pl.ds(at, PIECE), :]
        if k == 0:
            own_ref[...] = part
        else:
            high = part.astype(BF)
            sends[k - 1][0:PIECE, :] = high
            sends[k - 1][PIECE : 2 * PIECE, :] = (part - high.astype(F32)).astype(BF)


def two_part(ref):
    return ref[0:PIECE, :].astype(F32) + ref[PIECE : 2 * PIECE, :].astype(F32)


def piece_kernel(flags, own_ref, a_ref, b_ref, c_ref, in_ref, cols_ref, rows_ref, both_ref):
    part = (own_ref[...] + two_part(a_ref)) + (two_part(b_ref) + two_part(c_ref))
    high = part.astype(BF)
    both_ref[0:PIECE, :] = high
    both_ref[PIECE : 2 * PIECE, :] = (part - high.astype(F32)).astype(BF)
    for ref, line in ((cols_ref, in_ref[1]), (rows_ref, in_ref[0])):
        ref[0 : 2 * PIECE, :] = both_ref[...]
        ref[2 * PIECE : 2 * PIECE + TS, :] = line


def exchange_and_sum(flags, inner, outer, windows, grad_pre):
    own, send = call(
        tap_kernel, [((HALF, C), F32), ((HALF + STRIPS, C), BF)], 30, flags, windows, grad_pre, outer,
        scratch=[pltpu.VMEM((PADDED, C), F32)],
    )
    piece, a, b, c, strips = call(
        half_kernel, [((QUARTER, C), F32)] + [((QUARTER + 2 * STRIPS, C), BF)] * 3 + [((2 * STRIPS, C), BF)],
        24, flags, own, other_core(send), outer, scratch=[pltpu.VMEM((HALF, C), F32)],
    )
    own, out, d, e, f = call(
        quarter_kernel, [((PIECE, C), F32), ((2 * TS, C), BF)] + [((2 * PIECE + 2 * TS, C), BF)] * 3,
        24, flags, piece, strips, along_first(a, 1), along_first(b, 2), along_first(c, 3),
        scratch=[pltpu.VMEM((QUARTER, C), F32)],
    )
    d, e, f = along_second(d, 1), along_second(e, 2), along_second(f, 3)
    cols, rows, both = call(
        piece_kernel, [((2 * PIECE + TS, C), BF)] * 2 + [((2 * PIECE, C), BF)], 24, flags, own, d, e, f, inner
    )
    return (both, along_tile(cols, 1), along_tile(rows, 2), along_tile(both, 3)), (out, d, e, f)


LINES = [jax.ShapeDtypeStruct((2, TS, C), BF), jax.ShapeDtypeStruct((STRIPS, C), BF)]


def field_kernel(flags, mark_ref, a_ref, b_ref, c_ref, d_ref, field_ref, inner_ref, outer_ref):
    total = a_ref[...].astype(F32) + b_ref[...].astype(F32) + c_ref[...].astype(F32) + d_ref[...].astype(F32)
    outer_ref[2 * TS : STRIPS, :] = mark_ref[...]
    field_ref[...] = total.astype(BF)
    grid = total.reshape(TS, TS, C)
    split_lines(flags, total[0:TS], total[PIX - TS : PIX], grid[:, 0, :], grid[:, TS - 1, :], inner_ref, outer_ref)


def make_field(flags, marks, parts):
    return pl.pallas_call(
        field_kernel,
        out_shape=[jax.ShapeDtypeStruct((PIX, C), BF)] + LINES,
        in_specs=[SM] + [VM] * 5,
        out_specs=[VM] * 3,
        compiler_params=params(24),
        cost_estimate=cost(2**20, 3 * 2**20),
    )(flags, marks, *parts)


def conv_kernel(flags, field_ref, mark_ref, rows_ref, cols_ref, s0_ref, s1_ref, s2_ref, s3_ref, w_ref, bias_ref, cot_ref,
                act_ref, gp_ref, p_ref, mid_ref, inner_ref, outer_ref, q_ref, gf_ref):
    n = 34 * TS
    north, south, west, east = join_lines(flags, rows_ref[...], cols_ref[...], (s0_ref, s1_ref, s2_ref, s3_ref))
    outer_ref[2 * TS : STRIPS, :] = mark_ref[...]
    zero = jnp.zeros((1, C), F32)
    p_ref[1, 0:TS, :] = north.astype(BF)
    p_ref[1, TS : TS + PIX, :] = field_ref[...]
    p_ref[1, TS + PIX : n, :] = south.astype(BF)
    x = p_ref[1].astype(F32)
    col = lax.broadcasted_iota(I32, (n, C), 0) % TS
    west = jnp.concatenate([zero, west, zero])
    east = jnp.concatenate([zero, east, zero])
    p_ref[0] = jnp.where(col == 0, spread_rows(west), pltpu.roll(x, 1, 0)).astype(BF)
    p_ref[2] = jnp.where(col == TS - 1, spread_rows(east), pltpu.roll(x, n - 1, 0)).astype(BF)
    step = 256
    q_ref[1, 0 : 2 * TS, :] = jnp.zeros((2 * TS, C), BF)
    q_ref[1, 2 * TS + PIX : 4 * TS + PIX, :] = jnp.zeros((2 * TS, C), BF)
    for m in range(PIX // step):
        rows = slice(m * step, (m + 1) * step)
        pre = jnp.broadcast_to(bias_ref[...], (step, C))
        for a in range(3):
            for b in range(3):
                pre = pre + jnp.dot(
                    p_ref[b, a * TS + m * step : a * TS + (m + 1) * step, :], w_ref[a, b], preferred_element_type=F32
                )
        cdf = 0.5 * (1.0 + lax.erf(pre * root_half))
        act_ref[rows, :] = (pre * cdf).astype(BF)
        slope = cdf + pre * inv_root_two_pi * jnp.exp(-0.5 * pre * pre)
        g = (cot_ref[rows, :].astype(F32) * slope).astype(BF)
        gp_ref[rows, :] = g
        q_ref[1, 2 * TS + m * step : 2 * TS + (m + 1) * step, :] = g
        gf_ref[rows, :] = g.astype(F32)
    nq = 36 * TS
    y = q_ref[1].astype(F32)
    colq = lax.broadcasted_iota(I32, (nq, C), 0) % TS
    q_ref[0] = jnp.where(colq == TS - 1, 0.0, pltpu.roll(y, nq - 1, 0)).astype(BF)
    q_ref[2] = jnp.where(colq == 0, 0.0, pltpu.roll(y, 1, 0)).astype(BF)

    def back(r0, rows):
        acc = jnp.zeros((rows, C), F32)
        for a in range(3):
            for b in range(3):
                first = (2 - a) * TS + r0
                acc = acc + lax.dot_general(q_ref[b, first : first + rows, :], w_ref[a, b], NT, preferred_element_type=F32)
        return acc

    rid = lax.broadcasted_iota(I32, (TS, C), 0)
    sides = []
    for c, b in ((0, 0), (TS - 1, 2)):
        e = gf_ref[...].reshape(TS, TS, C)[:, c, :]
        up = jnp.where(rid == TS - 1, 0.0, pltpu.roll(e, TS - 1, 0))
        down = jnp.where(rid == 0, 0.0, pltpu.roll(e, 1, 0))
        acc = jnp.zeros((TS, C), F32)
        for a, v in ((0, up), (1, e), (2, down)):
            acc = acc + lax.dot_general(v.astype(BF), w_ref[a, b], NT, preferred_element_type=F32)
        sides.append(acc)
    split_lines(flags, back(0, TS), back(33 * TS, TS), sides[0], sides[1], inner_ref, outer_ref)
    for m in range(PIX // step):
        mid_ref[m * step : (m + 1) * step, :] = back(TS + m * step, step)


def conv(flags, field, marks, edges, w, bias, cot):
    return pl.pallas_call(
        conv_kernel,
        out_shape=[
            jax.ShapeDtypeStruct((PIX, C), BF),
            jax.ShapeDtypeStruct((PIX, C), BF),
            jax.ShapeDtypeStruct((3, 34 * TS, C), BF),
            jax.ShapeDtypeStruct((PIX, C), F32),
        ] + LINES,
        in_specs=[SM] + [VM] * 11,
        out_specs=[VM] * 6,
        scratch_shapes=[pltpu.VMEM((3, 36 * TS, C), BF), pltpu.VMEM((PIX, C), F32)],
        compiler_params=params(40),
        cost_estimate=cost(2**29, 2**19),
    )(flags, field, marks, *edges, w, bias, cot)


def total_kernel(flags, mid_ref, y1_ref, y2_ref, s0_ref, s1_ref, s2_ref, s3_ref, out_ref):
    cols = y1_ref[2 * PIECE : 2 * PIECE + TS, :]
    rows = y2_ref[2 * PIECE : 2 * PIECE + TS, :]
    north, south, west, east = join_lines(flags, rows, cols, (s0_ref, s1_ref, s2_ref, s3_ref))
    col = lax.broadcasted_iota(I32, (PIX, C), 0) % TS
    x = mid_ref[...]
    x = x + jnp.where(col == 0, spread_rows(west), 0.0) + jnp.where(col == TS - 1, spread_rows(east), 0.0)
    out_ref[...] = x.astype(BF)
    out_ref[0:TS, :] = (x[0:TS] + north).astype(BF)
    out_ref[PIX - TS : PIX, :] = (x[PIX - TS : PIX] + south).astype(BF)


def piece_sum_kernel(flags, y0_ref, y1_ref, y2_ref, y3_ref, taps_ref):
    taps_ref[...] = ((two_part(y0_ref) + two_part(y1_ref)) + (two_part(y2_ref) + two_part(y3_ref))).astype(BF)


def join_kernel(flags, *refs):
    out_ref = refs[-1]
    size = refs[0].shape[0]
    for k in range(4):
        out_ref[k * size : (k + 1) * size, :] = refs[k][...]


def joined(flags, parts, after, hold=()):
    size = parts[0].shape[0]
    return call(join_kernel, [((4 * size, C), BF)], 24, flags, *parts, after=after, hold=hold)[0]


def place_kernel(flags, own_ref, twin_ref, taps_ref, bias_ref, all_ref):
    face = flags[FACE]
    for c, ref in ((0, own_ref), (1, twin_ref)):
        for k in range(16):
            core, first, second = line_places(jnp.bitwise_xor(face, c))
            at = core * HALF + jnp.bitwise_xor(first, k >> 2) * QUARTER + jnp.bitwise_xor(second, k & 3) * PIECE
            all_ref[pl.ds(pl.multiple_of(at, 16), PIECE), :] = ref[k * PIECE : (k + 1) * PIECE, :].astype(F32)
    taps_ref[...] = all_ref[0:TAPS, :]
    bias_ref[...] = all_ref[TAPS : TAPS + 8, :][0:1, :]


def place_taps(flags, own, twin):
    taps, bias = call(
        place_kernel, [((TAPS, C), F32), ((1, C), F32)], 24, flags, own, twin, scratch=[pltpu.VMEM((PADDED, C), F32)]
    )
    return taps.reshape(3, 3, C, C), bias[0]


def shards(latlon, send_rows, send_count, interp_slot, interp_weight, outer_partner, outer_side, outer_flip,
           conv_weight, conv_bias, cotangent):
    faces = lax.axis_size("face")
    face = lax.axis_index("face")
    j = lax.axis_index("tile")
    steps = jnp.arange(4, dtype=I32)
    owner = j ^ steps
    group = jnp.concatenate([4 + j - owner, (j - owner) % 8])

    mine = jnp.concatenate([interp_slot.T.astype(F32), interp_weight.T])
    trio = jnp.stack([mine, from_face(mine, 1, faces), from_face(mine, -1, faces)])
    ask = [trio] + [along_tile(trio, k) for k in (1, 2, 3)]
    live = jnp.arange(CAP, dtype=I32)[None, :] < send_count[0][:, None]
    idx = jnp.where(live, send_rows[0], -1)[group]
    idx_cols = idx.T

    goal = outer_partner[0, 0] * 2 + outer_side[0, 0]
    marks = jnp.broadcast_to(jnp.repeat(goal, MARK // 2)[:, None], (MARK, C)).astype(BF)
    corner = jnp.stack([(j // 2 == 0), (j % 2 == 0)])
    whose = jnp.where(owner <= j, 1, 2)
    flags = jnp.concatenate(
        [jnp.stack([face, j]), outer_flip[0, 0], corner.astype(I32), group, jnp.zeros((4,), I32), whose]
    ).astype(I32)

    far = [None] * 4

    ask = ask + ask
    got6, got5 = gather_rows((6, 5), idx_cols, latlon)
    part, done = mix(flags, 6, ask[6], got6, [ask[1], ask[3]])
    far[2] = to_far(part, 2, faces)
    part, done = mix(flags, 5, ask[5], got5, [done])
    far[1] = to_far(part, 1, faces)
    part, done = partial_sum(flags, 7, idx_cols, latlon, ask[7], after=[done])
    far[3] = to_far(part, 3, faces)
    part, done = partial_sum(flags, 2, idx_cols, latlon, ask[2], far[2], [done])
    across = along_tile(part, 2)
    part, done = partial_sum(flags, 4, idx_cols, latlon, ask[4], after=[done])
    far[0] = to_far(part, 0, faces)
    part, done = partial_sum(flags, 1, idx_cols, latlon, ask[1], far[1], [done])
    up = along_tile(part, 1)
    part, done = partial_sum(flags, 3, idx_cols, latlon, ask[3], far[3], [done])
    down = along_tile(part, 3)
    part, done = partial_sum(flags, 0, idx_cols, latlon, ask[0], far[0], [done], [across])
    moved = [across, up, down]
    field, inner, outer = make_field(flags, marks, [part] + moved)
    edges = exchange(flags, inner, outer)
    activated, grad_pre, windows, mid, inner, outer = conv(
        flags, field, marks, edges, conv_weight, conv_bias[None, :], cotangent
    )
    lines, strips = exchange_and_sum(flags, inner, outer, windows, grad_pre)
    whole, = call(
        total_kernel, [((PIX, C), BF)], 24, flags, mid, lines[1], lines[2], *strips, after=[lines[3]]
    )
    up = along_tile(whole, 1)
    down = along_tile(whole, 3)
    far0 = from_far(whole, 0, faces)
    rows, done = row_grads(flags, idx, (0,), (ask[0],), (whole,), None, F32)
    rows, done = row_grads(flags, idx, (4,), (ask[4],), (far0,), rows, F32)
    taps, = call(piece_sum_kernel, [((PIECE, C), BF)], 24, flags, *lines, after=[done])
    moved = [along_second(taps, k) for k in (1, 2, 3)]
    up, down, whole = tied([up, down, whole], [done, *moved])
    across = along_tile(whole, 2)
    far1 = from_far(up, 1, faces)
    far3 = from_far(down, 3, faces)
    rows, done = row_grads(flags, idx, (1, 3), (ask[1], ask[3]), (up, down), rows, F32)
    across, = tied([across], [done])
    far2 = from_far(across, 2, faces)
    line = joined(flags, [taps] + moved, [done])
    moved = [along_first(line, k) for k in (1, 2, 3)]
    rows, done = row_grads(flags, idx, (5, 7), (ask[5], ask[7]), (far1, far3), rows, F32)
    taps = joined(flags, [line] + moved, [done], [far2])
    twin = other_core(taps)
    grad_latlon, done = row_grads(flags, idx, (2, 6), (ask[2], ask[6]), (across, far2), rows, BF)
    grad_weight, grad_bias = place_taps(flags, taps, twin)
    return activated, grad_latlon, grad_weight, grad_bias


def solution(mesh):
    both = ("face", "tile")
    placed = (
        P(both, None), P(both, None, None), P(both, None), P(both, None), P(both, None),
        P("face", "tile", None), P("face", "tile", None), P("face", "tile", None), P(), P(), P(both, None),
    )
    return jax.shard_map(
        shards, mesh=mesh, in_specs=placed, out_specs=(P(both, None), P(both, None), P(), P()), check_vma=False
    )
```

```python
import functools
import jax
import jax.numpy as jnp
from jax import lax
from jax.experimental import pallas as pl
from jax.experimental.pallas import tpu as pltpu
from jax.sharding import PartitionSpec as P

BF = jnp.bfloat16
F32 = jnp.float32
I16 = jnp.int16
I32 = jnp.int32
AXES = ("face", "tile")
TS = 32
PIX = 1024
CAP = 1024
ROWS = 4096
C = 256
MT = 512
KC = 256

FACE, TILE, FLIP, TOP, LEFT, GROUP, WHOSE = 0, 1, 2, 4, 5, 6, 14

root_half = 0.7071067811865476
inv_root_two_pi = 0.3989422804014327
VM = pl.BlockSpec(memory_space=pltpu.VMEM)
SM = pl.BlockSpec(memory_space=pltpu.SMEM)
HB = pl.BlockSpec(memory_space=pl.ANY)
NT = (((1,), (1,)), ((), ()))


def params(mib):
    return pltpu.CompilerParams(vmem_limit_bytes=mib * 2**20)


def cost(flops, size):
    return pl.CostEstimate(flops=flops, bytes_accessed=size, transcendentals=0)


def far_face(j, k):
    return 1 if j ^ k <= j else -1


def to_far(value, k, faces):
    pairs = []
    for face in range(faces):
        for j in range(4):
            pairs.append((face * 4 + j, (face + far_face(j, k)) % faces * 4 + j))
    return lax.ppermute(value, AXES, pairs)


def from_far(value, k, faces):
    pairs = []
    for face in range(faces):
        for j in range(4):
            pairs.append(((face + far_face(j, k)) % faces * 4 + j, face * 4 + j))
    return lax.ppermute(value, AXES, pairs)


def from_face(value, step, faces):
    return lax.ppermute(value, "face", [((i + step) % faces, i) for i in range(faces)])


def along_tile(value, k):
    return lax.ppermute(value, "tile", [(i, i ^ k) for i in range(4)])


def first_step(i):
    return 2 if i & 1 else 8


def second_step(i):
    return 8 if i & 1 else 2


def along_first(value, k):
    return lax.ppermute(value, "face", [(i, i ^ (k * first_step(i))) for i in range(32)])


def along_second(value, k):
    return lax.ppermute(value, "face", [(i, i ^ (k * second_step(i))) for i in range(32)])


def other_core(value):
    return lax.ppermute(value, "face", [(i, i ^ 1) for i in range(32)])


def gate(value, after):
    return lax.optimization_barrier((value, after))


def lanes_iota(shape, dim, dtype):
    return lax.broadcasted_iota(I32, shape, dim).astype(dtype)


def pick_rows(want, table_ref):
    base = lanes_iota((MT, KC), 1, I16)
    one = jnp.ones((MT, KC), BF)
    zero = jnp.zeros((MT, KC), BF)
    want = jnp.concatenate([jnp.broadcast_to(want, (MT, 128)).astype(I16)] * (KC // 128), axis=1)
    acc = jnp.zeros((MT, C), F32)
    for k in range(ROWS // KC):
        hot = jnp.where(want == base + jnp.asarray(k * KC, I16), one, zero)
        acc = acc + jnp.dot(hot, table_ref[k * KC : (k + 1) * KC, :], preferred_element_type=F32)
    return acc.astype(BF)


SUB = 64


def weigh(first, ask, w_ref):
    base = lanes_iota((SUB, 128), 1, I16)
    zero = jnp.zeros((SUB, 128), BF)
    row = lax.broadcasted_iota(I32, (8, PIX), 0)
    ask = jnp.where(row < 4, ask - first, ask).T
    for p in range(0, PIX, SUB):
        slots = [jnp.broadcast_to(ask[p : p + SUB, k : k + 1], (SUB, 128)).astype(I32).astype(I16) for k in range(4)]
        scale = [jnp.broadcast_to(ask[p : p + SUB, 4 + k : 5 + k], (SUB, 128)).astype(BF) for k in range(4)]
        for q in range(0, CAP, 128):
            here = base + jnp.asarray(q, I16)
            w = jnp.where(slots[0] == here, scale[0], zero)
            for k in range(1, 4):
                w = w + jnp.where(slots[k] == here, scale[k], zero)
            w_ref[p : p + SUB, q : q + 128] = w


def sum_kernel(which, has_add, given, flags, *refs):
    out_ref, done_ref = refs[-4:-2] if not given else refs[-3:-1]
    w_ref = refs[-1]
    if given:
        got_ref, ask_ref = refs[:2]
    else:
        idx_ref, table_ref, ask_ref = refs[:3]
        got_ref = refs[-2]
    done_ref[...] = jnp.zeros_like(done_ref)
    weigh((flags[GROUP + which] * CAP).astype(F32), ask_ref[flags[WHOSE + which]], w_ref)
    if not given:
        for m in range(0, CAP, MT):
            got_ref[m : m + MT, :] = pick_rows(idx_ref[m : m + MT, which : which + 1], table_ref)
    for m in range(0, PIX, MT):
        acc = refs[3][m : m + MT, :].astype(F32) if has_add else jnp.zeros((MT, C), F32)
        for q in range(0, CAP, KC):
            acc = acc + jnp.dot(w_ref[m : m + MT, q : q + KC], got_ref[q : q + KC, :], preferred_element_type=F32)
        out_ref[m : m + MT, :] = acc.astype(BF)


def sum_call(flags, which, has_add, given, operands, after, hold):
    scratch = [] if given else [pltpu.VMEM((CAP, C), BF)]
    return pl.pallas_call(
        functools.partial(sum_kernel, which, has_add, given),
        out_shape=[jax.ShapeDtypeStruct((PIX, C), BF), jax.ShapeDtypeStruct((8, 128), F32)],
        in_specs=[SM] + [VM] * (len(operands) + len(after)) + [HB] * len(hold),
        out_specs=[VM, VM],
        scratch_shapes=scratch + [pltpu.VMEM((PIX, CAP), BF)],
        compiler_params=params(30),
        cost_estimate=cost(2**29, 2**19),
    )(flags, *operands, *after, *hold)


def partial_sum(flags, which, idx, table, ask, add=None, after=(), hold=()):
    adds = [] if add is None else [add]
    return sum_call(flags, which, bool(adds), False, [idx, table, ask, *adds], after, hold)


def gather_kernel(picks, idx_ref, table_ref, *outs):
    for b, out_ref in zip(picks, outs):
        for m in range(0, CAP, MT):
            out_ref[m : m + MT, :] = pick_rows(idx_ref[m : m + MT, b : b + 1], table_ref)


def gather_rows(picks, idx, table):
    n = len(picks)
    return pl.pallas_call(
        functools.partial(gather_kernel, picks),
        out_shape=[jax.ShapeDtypeStruct((CAP, C), BF)] * n,
        in_specs=[VM] * 2,
        out_specs=[VM] * n,
        compiler_params=params(24),
        cost_estimate=cost(n * 2**29, 2**19),
    )(idx, table)


def mix(flags, which, ask, got, after=()):
    return sum_call(flags, which, False, True, [got, ask], after, ())


PUT = 1024


def scatter_kernel(blocks, halves, has_add, flags, idx_ref, *rest):
    n = len(blocks)
    asks = rest[:n]
    rest = rest[n:]
    grads = []
    for h in halves:
        grads.append(rest[:h])
        rest = rest[h:]
    if has_add:
        add_ref = rest[0]
    out_ref, done_ref, slot_ref = rest[-3:]

    def spread(row, rows, dtype):
        tall = jnp.broadcast_to(row, (16, KC)).astype(dtype)
        return jnp.broadcast_to(tall[None], (rows // 16, 16, KC)).reshape(rows, KC)

    @pl.when(pl.program_id(0) == 0)
    def _():
        base = lanes_iota((MT, KC), 0, I16)
        zero = jnp.zeros((MT, KC), BF)
        for i in range(n):
            group = (flags[GROUP + blocks[i]] * CAP).astype(F32)
            who = flags[WHOSE + blocks[i]]

            def mixed(m, carry):
                first = group + (m * MT).astype(F32)
                acc = jnp.zeros((MT, C), F32)
                for q in range(PIX // KC):
                    lanes = slice(q * KC, (q + 1) * KC)
                    w = None
                    for k in range(4):
                        slots = spread((asks[i][who, k : k + 1, lanes] - first).astype(I32), MT, I16)
                        term = jnp.where(slots == base, spread(asks[i][who, 4 + k : 5 + k, lanes], MT, BF), zero)
                        w = term if w is None else w + term
                    part = PIX // halves[i]
                    ref = grads[i][q * KC // part]
                    at = q * KC % part
                    acc = acc + jnp.dot(w, ref[at : at + KC, :], preferred_element_type=F32)
                slot_ref[pl.ds(pl.multiple_of(i * CAP + m * MT, MT), MT), :] = acc.astype(BF)
                return carry

            lax.fori_loop(0, CAP // MT, mixed, 0)

    base = lanes_iota((PUT, KC), 0, I16)
    one = jnp.ones((PUT, KC), BF)
    zero = jnp.zeros((PUT, KC), BF)
    first = pl.program_id(0) * PUT
    acc = add_ref[...] if has_add else jnp.zeros((PUT, C), F32)
    for i in range(n):
        for q in range(CAP // KC):
            want = spread(idx_ref[blocks[i] : blocks[i] + 1, q * KC : (q + 1) * KC] - first, PUT, I16)
            hot = jnp.where(want == base, one, zero)
            at = i * CAP + q * KC
            acc = acc + jnp.dot(hot, slot_ref[at : at + KC, :], preferred_element_type=F32)
    out_ref[...] = acc.astype(out_ref.dtype)
    done_ref[...] = jnp.zeros_like(done_ref)


def row_grads(flags, idx, blocks, asks, grads, add, dtype, after=(), hold=()):
    n = len(blocks)
    has_add = add is not None
    grads = [g if isinstance(g, tuple) else (g,) for g in grads]
    halves = [len(g) for g in grads]
    whole = [idx, *asks] + [x for g in grads for x in g]
    tile = pl.BlockSpec((PUT, C), lambda m: (m, 0))
    specs = [SM] + [pl.BlockSpec(x.shape, lambda m, n=x.ndim: (0,) * n) for x in whole] + ([tile] if has_add else [])
    specs = specs + [VM] * len(after) + [HB] * len(hold)
    return pl.pallas_call(
        functools.partial(scatter_kernel, blocks, halves, has_add),
        grid=(ROWS // PUT,),
        out_shape=[jax.ShapeDtypeStruct((ROWS, C), dtype), jax.ShapeDtypeStruct((8, 128), F32)],
        in_specs=specs,
        out_specs=[tile, pl.BlockSpec((8, 128), lambda m: (0, 0))],
        scratch_shapes=[pltpu.VMEM((n * CAP, C), BF)],
        compiler_params=params(40),
        cost_estimate=cost(n * 2**29, 2**19),
    )(flags, *whole, *([add] if has_add else []), *after, *hold)


MARK = 16
STRIPS = 2 * TS + MARK
TAPS = 9 * C
PADDED = 2560
HALF, QUARTER, PIECE = PADDED // 2, PADDED // 8, PADDED // 32


def spread_rows(lines):
    rows = lines.shape[0]
    return jnp.broadcast_to(lines[:, None, :], (rows, TS, C)).reshape(rows * TS, C)


def split_lines(flags, north, south, west, east, inner_ref, outer_ref):
    top = flags[TOP] == 1
    left = flags[LEFT] == 1
    inner_ref[0] = jnp.where(top, south, north).astype(BF)
    inner_ref[1] = jnp.where(left, east, west).astype(BF)
    outer_ref[0:TS, :] = jnp.where(top, north, south).astype(BF)
    outer_ref[TS : 2 * TS, :] = jnp.where(left, west, east).astype(BF)


def join_lines(flags, in_rows, in_cols, parts):
    row = lax.broadcasted_iota(I32, (TS, TS), 0)
    col = lax.broadcasted_iota(I32, (TS, TS), 1)
    turn = (row + col == TS - 1).astype(BF)
    outer = []
    for s in range(2):
        line = jnp.zeros((TS, C), BF)
        for part in parts:
            at = part.shape[0] - 2 * TS + s * TS
            line = line + part[at : at + TS, :]
        back = jnp.dot(turn, line, preferred_element_type=F32)
        outer.append(jnp.where(flags[FLIP + s] == 1, back, line.astype(F32)))
    top = flags[TOP] == 1
    left = flags[LEFT] == 1
    in_rows = in_rows.astype(F32)
    in_cols = in_cols.astype(F32)
    north = jnp.where(top, outer[0], in_rows)
    south = jnp.where(top, in_rows, outer[0])
    west = jnp.where(left, outer[1], in_cols)
    east = jnp.where(left, in_cols, outer[1])
    return north, south, west, east


def call(kernel, outs, mib, flags, *operands, scratch=(), after=(), hold=()):
    n, m = len(operands), len(after) + len(hold)

    def body(flags, *refs):
        kernel(flags, *refs[:n], *refs[n + m :])

    return pl.pallas_call(
        body,
        out_shape=[jax.ShapeDtypeStruct(shape, dtype) for shape, dtype in outs],
        in_specs=[SM] + [VM] * (n + len(after)) + [HB] * len(hold),
        out_specs=[VM] * len(outs),
        scratch_shapes=list(scratch),
        compiler_params=params(mib),
        cost_estimate=cost(2**20, 2**20),
    )(flags, *operands, *after, *hold)


def tie_kernel(*refs):
    pass


def tied(values, after):
    n = len(values)
    return pl.pallas_call(
        tie_kernel,
        out_shape=[jax.ShapeDtypeStruct(x.shape, x.dtype) for x in values],
        in_specs=[HB] * n + [VM] * len(after),
        out_specs=[HB] * n,
        input_output_aliases={i: i for i in range(n)},
        compiler_params=params(1),
        cost_estimate=cost(2**10, 2**10),
    )(*values, *after)


def line_places(face):
    core = jnp.bitwise_and(face, 1)
    x = jnp.bitwise_and(lax.shift_right_logical(face, 1), 3)
    z = lax.shift_right_logical(face, 3)
    return core, jnp.where(core == 0, z, x), jnp.where(core == 0, x, z)


def pick_strips(flags, sets, outs):
    face = flags[FACE]
    step = jnp.where(jnp.bitwise_and(face, 1) == 0, 2, 8)
    zero = jnp.zeros((TS, C), F32)
    want = [[zero, zero] for _ in range(4)]
    for ref, at in sets:
        for core in range(2):
            base = at + core * STRIPS
            for s in range(2):
                strip = ref[base + s * TS : base + (s + 1) * TS, :].astype(F32)
                mark = ref[base + 2 * TS : base + STRIPS, :].astype(F32)[s * 8 : s * 8 + 1, :]
                mark = jnp.broadcast_to(mark, (TS, C))
                for k in range(4):
                    for slot in range(2):
                        place = (jnp.bitwise_xor(face, step * k) * 2 + slot).astype(F32)
                        want[k][slot] = jnp.where(mark == place, strip, want[k][slot])
    for k in range(4):
        ref, at = outs[k]
        for slot in range(2):
            ref[at + slot * TS : at + (slot + 1) * TS, :] = want[k][slot].astype(BF)


def route_kernel(flags, own_ref, a_ref, b_ref, c_ref, *outs):
    pick_strips(flags, [(r, 0) for r in (own_ref, a_ref, b_ref, c_ref)], [(r, 0) for r in outs])


def exchange(flags, inner, outer):
    rows = lax.ppermute(inner[0], "tile", [(i, i ^ 2) for i in range(4)])
    cols = lax.ppermute(inner[1], "tile", [(i, i ^ 1) for i in range(4)])
    both = jnp.concatenate([outer, other_core(outer)])
    sets = [along_first(both, k) for k in (1, 2, 3)]
    sets, rows, cols = lax.optimization_barrier((sets, rows, cols))
    ways = call(route_kernel, [((2 * TS, C), BF)] * 4, 24, flags, both, *sets)
    return [rows, cols, ways[0]] + [along_second(ways[k], k) for k in (1, 2, 3)]


def tap_kernel(flags, p_ref, gp_ref, outer_ref, own_ref, send_ref, all_ref):
    turned = gp_ref[...].T
    for a in range(3):
        for b in range(3):
            at = (a * 3 + b) * C
            part = jnp.dot(turned, p_ref[b, a * TS : a * TS + PIX, :], preferred_element_type=F32)
            all_ref[at : at + C, :] = part.T
    bias = jnp.sum(gp_ref[...].astype(F32), axis=0, keepdims=True)
    row = lax.broadcasted_iota(I32, (PADDED - TAPS, C), 0)
    all_ref[TAPS:PADDED, :] = jnp.where(row == 0, bias, 0.0)
    core = jnp.bitwise_and(flags[FACE], 1)
    own_ref[...] = all_ref[pl.ds(pl.multiple_of(core * HALF, 64), HALF), :]
    send_ref[0:HALF, :] = all_ref[pl.ds(pl.multiple_of((1 - core) * HALF, 64), HALF), :].astype(BF)
    send_ref[HALF : HALF + STRIPS, :] = outer_ref[...]


def half_kernel(flags, own_ref, got_ref, outer_ref, piece_ref, *rest):
    sends = rest[:3]
    strips_ref, all_ref = rest[3:]
    all_ref[...] = own_ref[...] + got_ref[0:HALF, :].astype(F32)
    strips_ref[0:STRIPS, :] = outer_ref[...]
    strips_ref[STRIPS : 2 * STRIPS, :] = got_ref[HALF : HALF + STRIPS, :]
    _, first, _ = line_places(flags[FACE])
    for k in range(4):
        at = pl.multiple_of(jnp.bitwise_xor(first, k) * QUARTER, 64)
        part = all_ref[pl.ds(at, QUARTER), :]
        if k == 0:
            piece_ref[...] = part
        else:
            sends[k - 1][0:QUARTER, :] = part.astype(BF)
            sends[k - 1][QUARTER : QUARTER + 2 * STRIPS, :] = strips_ref[...]


def quarter_kernel(flags, piece_ref, strips_ref, a_ref, b_ref, c_ref, own_ref, out_ref, *rest):
    sends = rest[:3]
    all_ref = rest[3]
    got = [r[0:QUARTER, :].astype(F32) for r in (a_ref, b_ref, c_ref)]
    all_ref[...] = (piece_ref[...] + got[0]) + (got[1] + got[2])
    pick_strips(
        flags,
        [(strips_ref, 0)] + [(r, QUARTER) for r in (a_ref, b_ref, c_ref)],
        [(out_ref, 0)] + [(r, 2 * PIECE) for r in sends],
    )
    _, _, second = line_places(flags[FACE])
    for k in range(4):
        at = pl.multiple_of(jnp.bitwise_xor(second, k) * PIECE, 16)
        part = all_ref[pl.ds(at, PIECE), :]
        if k == 0:
            own_ref[...] = part
        else:
            high = part.astype(BF)
            sends[k - 1][0:PIECE, :] = high
            sends[k - 1][PIECE : 2 * PIECE, :] = (part - high.astype(F32)).astype(BF)


def two_part(ref):
    return ref[0:PIECE, :].astype(F32) + ref[PIECE : 2 * PIECE, :].astype(F32)


def piece_kernel(flags, own_ref, a_ref, b_ref, c_ref, in_ref, cols_ref, rows_ref, both_ref):
    part = (own_ref[...] + two_part(a_ref)) + (two_part(b_ref) + two_part(c_ref))
    high = part.astype(BF)
    both_ref[0:PIECE, :] = high
    both_ref[PIECE : 2 * PIECE, :] = (part - high.astype(F32)).astype(BF)
    for ref, line in ((cols_ref, in_ref[1]), (rows_ref, in_ref[0])):
        ref[0 : 2 * PIECE, :] = both_ref[...]
        ref[2 * PIECE : 2 * PIECE + TS, :] = line


def exchange_and_sum(flags, inner, outer, windows, grad_pre):
    own, send = call(
        tap_kernel, [((HALF, C), F32), ((HALF + STRIPS, C), BF)], 30, flags, windows, grad_pre, outer,
        scratch=[pltpu.VMEM((PADDED, C), F32)],
    )
    piece, a, b, c, strips = call(
        half_kernel, [((QUARTER, C), F32)] + [((QUARTER + 2 * STRIPS, C), BF)] * 3 + [((2 * STRIPS, C), BF)],
        24, flags, own, other_core(send), outer, scratch=[pltpu.VMEM((HALF, C), F32)],
    )
    own, out, d, e, f = call(
        quarter_kernel, [((PIECE, C), F32), ((2 * TS, C), BF)] + [((2 * PIECE + 2 * TS, C), BF)] * 3,
        24, flags, piece, strips, along_first(a, 1), along_first(b, 2), along_first(c, 3),
        scratch=[pltpu.VMEM((QUARTER, C), F32)],
    )
    d, e, f = along_second(d, 1), along_second(e, 2), along_second(f, 3)
    cols, rows, both = call(
        piece_kernel, [((2 * PIECE + TS, C), BF)] * 2 + [((2 * PIECE, C), BF)], 24, flags, own, d, e, f, inner
    )
    return (both, along_tile(cols, 1), along_tile(rows, 2), along_tile(both, 3)), (out, d, e, f)


LINES = [jax.ShapeDtypeStruct((2, TS, C), BF), jax.ShapeDtypeStruct((STRIPS, C), BF)]


def field_kernel(flags, mark_ref, a_ref, b_ref, c_ref, d_ref, field_ref, inner_ref, outer_ref):
    total = a_ref[...].astype(F32) + b_ref[...].astype(F32) + c_ref[...].astype(F32) + d_ref[...].astype(F32)
    outer_ref[2 * TS : STRIPS, :] = mark_ref[...]
    field_ref[...] = total.astype(BF)
    grid = total.reshape(TS, TS, C)
    split_lines(flags, total[0:TS], total[PIX - TS : PIX], grid[:, 0, :], grid[:, TS - 1, :], inner_ref, outer_ref)


def make_field(flags, marks, parts):
    return pl.pallas_call(
        field_kernel,
        out_shape=[jax.ShapeDtypeStruct((PIX, C), BF)] + LINES,
        in_specs=[SM] + [VM] * 5,
        out_specs=[VM] * 3,
        compiler_params=params(24),
        cost_estimate=cost(2**20, 3 * 2**20),
    )(flags, marks, *parts)


def conv_kernel(flags, field_ref, mark_ref, rows_ref, cols_ref, s0_ref, s1_ref, s2_ref, s3_ref, w_ref, bias_ref, cot_ref,
                act_ref, gp_ref, p_ref, mid_ref, inner_ref, outer_ref, q_ref, gf_ref):
    n = 34 * TS
    north, south, west, east = join_lines(flags, rows_ref[...], cols_ref[...], (s0_ref, s1_ref, s2_ref, s3_ref))
    outer_ref[2 * TS : STRIPS, :] = mark_ref[...]
    zero = jnp.zeros((1, C), F32)
    p_ref[1, 0:TS, :] = north.astype(BF)
    p_ref[1, TS : TS + PIX, :] = field_ref[...]
    p_ref[1, TS + PIX : n, :] = south.astype(BF)
    x = p_ref[1].astype(F32)
    col = lax.broadcasted_iota(I32, (n, C), 0) % TS
    west = jnp.concatenate([zero, west, zero])
    east = jnp.concatenate([zero, east, zero])
    p_ref[0] = jnp.where(col == 0, spread_rows(west), pltpu.roll(x, 1, 0)).astype(BF)
    p_ref[2] = jnp.where(col == TS - 1, spread_rows(east), pltpu.roll(x, n - 1, 0)).astype(BF)
    step = 256
    q_ref[1, 0 : 2 * TS, :] = jnp.zeros((2 * TS, C), BF)
    q_ref[1, 2 * TS + PIX : 4 * TS + PIX, :] = jnp.zeros((2 * TS, C), BF)
    for m in range(PIX // step):
        rows = slice(m * step, (m + 1) * step)
        pre = jnp.broadcast_to(bias_ref[...], (step, C))
        for a in range(3):
            for b in range(3):
                pre = pre + jnp.dot(
                    p_ref[b, a * TS + m * step : a * TS + (m + 1) * step, :], w_ref[a, b], preferred_element_type=F32
                )
        cdf = 0.5 * (1.0 + lax.erf(pre * root_half))
        act_ref[rows, :] = (pre * cdf).astype(BF)
        slope = cdf + pre * inv_root_two_pi * jnp.exp(-0.5 * pre * pre)
        g = (cot_ref[rows, :].astype(F32) * slope).astype(BF)
        gp_ref[rows, :] = g
        q_ref[1, 2 * TS + m * step : 2 * TS + (m + 1) * step, :] = g
        gf_ref[rows, :] = g.astype(F32)
    nq = 36 * TS
    y = q_ref[1].astype(F32)
    colq = lax.broadcasted_iota(I32, (nq, C), 0) % TS
    q_ref[0] = jnp.where(colq == TS - 1, 0.0, pltpu.roll(y, nq - 1, 0)).astype(BF)
    q_ref[2] = jnp.where(colq == 0, 0.0, pltpu.roll(y, 1, 0)).astype(BF)

    def back(r0, rows):
        acc = jnp.zeros((rows, C), F32)
        for a in range(3):
            for b in range(3):
                first = (2 - a) * TS + r0
                acc = acc + lax.dot_general(q_ref[b, first : first + rows, :], w_ref[a, b], NT, preferred_element_type=F32)
        return acc

    rid = lax.broadcasted_iota(I32, (TS, C), 0)
    sides = []
    for c, b in ((0, 0), (TS - 1, 2)):
        e = gf_ref[...].reshape(TS, TS, C)[:, c, :]
        up = jnp.where(rid == TS - 1, 0.0, pltpu.roll(e, TS - 1, 0))
        down = jnp.where(rid == 0, 0.0, pltpu.roll(e, 1, 0))
        acc = jnp.zeros((TS, C), F32)
        for a, v in ((0, up), (1, e), (2, down)):
            acc = acc + lax.dot_general(v.astype(BF), w_ref[a, b], NT, preferred_element_type=F32)
        sides.append(acc)
    split_lines(flags, back(0, TS), back(33 * TS, TS), sides[0], sides[1], inner_ref, outer_ref)
    for m in range(PIX // step):
        mid_ref[m * step : (m + 1) * step, :] = back(TS + m * step, step)


def conv(flags, field, marks, edges, w, bias, cot):
    return pl.pallas_call(
        conv_kernel,
        out_shape=[
            jax.ShapeDtypeStruct((PIX, C), BF),
            jax.ShapeDtypeStruct((PIX, C), BF),
            jax.ShapeDtypeStruct((3, 34 * TS, C), BF),
            jax.ShapeDtypeStruct((PIX, C), F32),
        ] + LINES,
        in_specs=[SM] + [VM] * 11,
        out_specs=[VM] * 6,
        scratch_shapes=[pltpu.VMEM((3, 36 * TS, C), BF), pltpu.VMEM((PIX, C), F32)],
        compiler_params=params(40),
        cost_estimate=cost(2**29, 2**19),
    )(flags, field, marks, *edges, w, bias, cot)


def total_kernel(flags, mid_ref, y1_ref, y2_ref, s0_ref, s1_ref, s2_ref, s3_ref, out_ref):
    cols = y1_ref[2 * PIECE : 2 * PIECE + TS, :]
    rows = y2_ref[2 * PIECE : 2 * PIECE + TS, :]
    north, south, west, east = join_lines(flags, rows, cols, (s0_ref, s1_ref, s2_ref, s3_ref))
    col = lax.broadcasted_iota(I32, (PIX, C), 0) % TS
    x = mid_ref[...]
    x = x + jnp.where(col == 0, spread_rows(west), 0.0) + jnp.where(col == TS - 1, spread_rows(east), 0.0)
    out_ref[...] = x.astype(BF)
    out_ref[0:TS, :] = (x[0:TS] + north).astype(BF)
    out_ref[PIX - TS : PIX, :] = (x[PIX - TS : PIX] + south).astype(BF)


def piece_sum_kernel(flags, y0_ref, y1_ref, y2_ref, y3_ref, taps_ref):
    taps_ref[...] = ((two_part(y0_ref) + two_part(y1_ref)) + (two_part(y2_ref) + two_part(y3_ref))).astype(BF)


def join_kernel(flags, *refs):
    out_ref = refs[-1]
    size = refs[0].shape[0]
    for k in range(4):
        out_ref[k * size : (k + 1) * size, :] = refs[k][...]


def joined(flags, parts, after, hold=()):
    size = parts[0].shape[0]
    return call(join_kernel, [((4 * size, C), BF)], 24, flags, *parts, after=after, hold=hold)[0]


def place_kernel(flags, own_ref, twin_ref, taps_ref, bias_ref, all_ref):
    face = flags[FACE]
    for c, ref in ((0, own_ref), (1, twin_ref)):
        for k in range(16):
            core, first, second = line_places(jnp.bitwise_xor(face, c))
            at = core * HALF + jnp.bitwise_xor(first, k >> 2) * QUARTER + jnp.bitwise_xor(second, k & 3) * PIECE
            all_ref[pl.ds(pl.multiple_of(at, 16), PIECE), :] = ref[k * PIECE : (k + 1) * PIECE, :].astype(F32)
    taps_ref[...] = all_ref[0:TAPS, :]
    bias_ref[...] = all_ref[TAPS : TAPS + 8, :][0:1, :]


def place_taps(flags, own, twin):
    taps, bias = call(
        place_kernel, [((TAPS, C), F32), ((1, C), F32)], 24, flags, own, twin, scratch=[pltpu.VMEM((PADDED, C), F32)]
    )
    return taps.reshape(3, 3, C, C), bias[0]


def shards(latlon, send_rows, send_count, interp_slot, interp_weight, outer_partner, outer_side, outer_flip,
           conv_weight, conv_bias, cotangent):
    faces = lax.axis_size("face")
    face = lax.axis_index("face")
    j = lax.axis_index("tile")
    steps = jnp.arange(4, dtype=I32)
    owner = j ^ steps
    group = jnp.concatenate([4 + j - owner, (j - owner) % 8])

    mine = jnp.concatenate([interp_slot.T.astype(F32), interp_weight.T])
    trio = jnp.stack([mine, from_face(mine, 1, faces), from_face(mine, -1, faces)])
    ask = [trio] + [along_tile(trio, k) for k in (1, 2, 3)]
    live = jnp.arange(CAP, dtype=I32)[None, :] < send_count[0][:, None]
    idx = jnp.where(live, send_rows[0], -1)[group]
    idx_cols = idx.T

    goal = outer_partner[0, 0] * 2 + outer_side[0, 0]
    marks = jnp.broadcast_to(jnp.repeat(goal, MARK // 2)[:, None], (MARK, C)).astype(BF)
    corner = jnp.stack([(j // 2 == 0), (j % 2 == 0)])
    whose = jnp.where(owner <= j, 1, 2)
    flags = jnp.concatenate(
        [jnp.stack([face, j]), outer_flip[0, 0], corner.astype(I32), group, jnp.zeros((4,), I32), whose]
    ).astype(I32)

    far = [None] * 4

    ask = ask + ask
    got6, got5 = gather_rows((6, 5), idx_cols, latlon)
    part, done = mix(flags, 6, ask[6], got6, [ask[1], ask[3]])
    far[2] = to_far(part, 2, faces)
    part, done = mix(flags, 5, ask[5], got5, [done])
    far[1] = to_far(part, 1, faces)
    part, done = partial_sum(flags, 7, idx_cols, latlon, ask[7], after=[done])
    far[3] = to_far(part, 3, faces)
    part, done = partial_sum(flags, 2, idx_cols, latlon, ask[2], far[2], [done])
    across = along_tile(part, 2)
    part, done = partial_sum(flags, 4, idx_cols, latlon, ask[4], after=[done])
    far[0] = to_far(part, 0, faces)
    part, done = partial_sum(flags, 1, idx_cols, latlon, ask[1], far[1], [done])
    up = along_tile(part, 1)
    part, done = partial_sum(flags, 3, idx_cols, latlon, ask[3], far[3], [done])
    down = along_tile(part, 3)
    part, done = partial_sum(flags, 0, idx_cols, latlon, ask[0], far[0], [done], [across])
    moved = [across, up, down]
    field, inner, outer = make_field(flags, marks, [part] + moved)
    edges = exchange(flags, inner, outer)
    activated, grad_pre, windows, mid, inner, outer = conv(
        flags, field, marks, edges, conv_weight, conv_bias[None, :], cotangent
    )
    lines, strips = exchange_and_sum(flags, inner, outer, windows, grad_pre)
    whole, = call(
        total_kernel, [((PIX, C), BF)], 24, flags, mid, lines[1], lines[2], *strips, after=[lines[3]]
    )
    up = along_tile(whole, 1)
    down = along_tile(whole, 3)
    far0 = from_far(whole, 0, faces)
    rows, done = row_grads(flags, idx, (0,), (ask[0],), (whole,), None, F32)
    taps, = call(piece_sum_kernel, [((PIECE, C), BF)], 24, flags, *lines, after=[done])
    rows, done = row_grads(flags, idx, (4,), (ask[4],), (far0,), rows, F32)
    moved = [along_second(taps, k) for k in (1, 2, 3)]
    up, down, whole = tied([up, down, whole], [done, *moved])
    across = along_tile(whole, 2)
    far1 = from_far(up, 1, faces)
    far3 = from_far(down, 3, faces)
    rows, done = row_grads(flags, idx, (1, 3), (ask[1], ask[3]), (up, down), rows, F32)
    across, = tied([across], [done])
    far2 = from_far(across, 2, faces)
    line = joined(flags, [taps] + moved, [done])
    moved = [along_first(line, k) for k in (1, 2, 3)]
    rows, done = row_grads(flags, idx, (5, 7), (ask[5], ask[7]), (far1, far3), rows, F32)
    taps = joined(flags, [line] + moved, [done], [far2])
    twin = other_core(taps)
    grad_latlon, done = row_grads(flags, idx, (2, 6), (ask[2], ask[6]), (across, far2), rows, BF)
    grad_weight, grad_bias = place_taps(flags, taps, twin)
    return activated, grad_latlon, grad_weight, grad_bias


def solution(mesh):
    both = ("face", "tile")
    placed = (
        P(both, None), P(both, None, None), P(both, None), P(both, None), P(both, None),
        P("face", "tile", None), P("face", "tile", None), P("face", "tile", None), P(), P(), P(both, None),
    )
    return jax.shard_map(
        shards, mesh=mesh, in_specs=placed, out_specs=(P(both, None), P(both, None), P(), P()), check_vma=False
    )
```
